1024 devices in a mesh: patch: 64 (over z_hi, x, y), ens: 16 (over z_lo, core).
Axes of the slice: x: 4, y: 8, z: 16 (z_hi: 2, z_lo: 8; z = z_hi * 8 + z_lo), core: 2. Of those that a mesh axis runs over, the one named last changes fastest.
Arguments:
- pred: bfloat16 [16, 8192, 128], P('ens', 'patch'), may hold values from -6 to 6
- target: bfloat16 [8192, 128], P('patch'), may hold values from -6 to 6
- h1: bfloat16 [16, 8192, 1024], P('ens', 'patch'), may hold values from -6 to 6
- w1: bfloat16 [1024, 1024], replicated, may hold values from -0.1875 to 0.1875
- w2: bfloat16 [1024, 128], replicated, may hold values from -0.5 to 0.5
- neighbours: int32 [64, 256, 6], P('patch'), may hold values from 0 to 255, as said below
- rotations: int32 [64, 256, 6], P('patch'), may hold values from 0 to 7, as said below
Outputs:
- grad_h1: bfloat16 [16, 8192, 1024], P('ens', 'patch')
The draws below stay inside these ranges and needn't reach their ends.
Inputs may be any that keep to these rules, and one draw needn't show every extreme that they name: Row l of patch p's table lists the neighbours of vertex p * 128 - 2 * 32 + l as window rows; every neighbour lies 1 to 32 vertices away in vertex order, and column 0 exactly 32. All tables agree on every vertex that they share. Rows of vertices outside the mesh, and neighbours outside the window, name the row itself. `rotations`: tables of all patches agree on every vertex that they share.
All inputs are finite; a program needn't handle non-finite values.
Results may differ from the reference program's by a relative error of at most 0.023.
Values may be sent and summed in bfloat16 or wider, within the bound.
A program may use at most 32 MiB of HBM per device.

```python
import math
import jax
import jax.numpy as jnp
from jax import lax

C = 1024
COUT = 128
K = 6
H = 32
R = 128
MEMBERS = 16
PATCHES = 64
NV = 8192
RW = 256


def global_links(key):
    key_dist, key_side = jax.random.split(jax.random.fold_in(key, 11))
    vertex = jnp.arange(NV, dtype=jnp.int32)[:, None]
    distance = jax.random.randint(key_dist, (NV, K), 1, H + 1)
    column_ids = jnp.arange(K, dtype=jnp.int32)[None, :]
    distance = jnp.where(column_ids == 0, H, distance)
    direction = jax.random.randint(key_side, (NV, K), 0, 2) * 2 - 1
    linked = vertex + distance * direction
    outside = (linked < 0) | (linked >= NV)
    return jnp.where(outside, vertex - distance * direction, linked)


def window_rows():
    patch_ids = jnp.arange(PATCHES, dtype=jnp.int32)[:, None]
    local_rows = jnp.arange(RW, dtype=jnp.int32)[None, :]
    global_rows = patch_ids * R - 2 * H + local_rows
    return (global_rows, local_rows)


def draw_neighbours(key, part):
    targets_global = global_links(key)
    global_rows, local_rows = window_rows()
    valid = (global_rows >= 0) & (global_rows < NV)
    source_row = jnp.clip(global_rows, 0, NV - 1)
    linked = targets_global[source_row]
    window_start = global_rows - local_rows
    local_link = linked - window_start[:, :, None]
    inside = valid[:, :, None] & (local_link >= 0) & (local_link < RW)
    itself = jnp.broadcast_to(local_rows[:, :, None], (PATCHES, RW, K))
    return jnp.where(inside, local_link, itself).astype(jnp.int32)


def draw_rotations(key, part):
    turns = jax.random.randint(jax.random.fold_in(key, 23), (NV, K), 0, 8)
    global_rows, local_rows = window_rows()
    source_row = jnp.clip(global_rows, 0, NV - 1)
    return turns[source_row].astype(jnp.int32)


def block_scale(own_key, shape, shards, low, high):
    def one(dim, shards_of):
        steps = jax.random.uniform(jax.random.fold_in(jax.random.fold_in(own_key, 6), dim), (shards_of,), jnp.float32, low / len(shards), high / len(shards))
        return jnp.repeat(jnp.exp(steps), shape[dim] // shards_of).reshape((-1,) + (1,) * (len(shape) - dim - 1))

    factor_of = one(*shards[0])
    for cut in shards[1:]:
        factor_of = factor_of * one(*cut)
    return factor_of


def normal_values(rng, dims, width, bound, pieces=(), held_as=jnp.bfloat16):
    array = jax.random.normal(rng, dims, jnp.float32) * width
    if len(pieces) > 0:
        array = block_scale(rng, dims, pieces, -0.22, 0.18) * array
    return jnp.clip(array, min=-bound, max=bound).astype(held_as)


def setup_inputs(seed: int = 0) -> dict:
    streams_of = jax.random.split(jax.random.key(seed), 8)
    return {
        "pred": normal_values(streams_of[0], (MEMBERS, NV, COUT), 1.0, 6.0, ((0, 16), (1, 64))),
        "target": normal_values(streams_of[1], (NV, COUT), 1.0, 6.0, ((0, 64),)),
        "h1": normal_values(streams_of[2], (MEMBERS, NV, C), 1.0, 6.0, ((0, 16), (1, 64))),
        "w1": normal_values(streams_of[3], (C, C), C ** -0.5, 0.1875),
        "w2": normal_values(streams_of[4], (C, COUT), COUT ** -0.5, 0.5),
        "neighbours": draw_neighbours(jax.random.fold_in(streams_of[7], 71), 0),
        "rotations": draw_rotations(jax.random.fold_in(streams_of[7], 71), 0),
    }


angle_step = 2.0 * math.pi / 8.0


def rotate_pairs(block, cosines, sines):
    half_width = block.shape[-1] // 2
    real_part = block[:, :half_width]
    imag_part = block[:, half_width:]
    return jnp.concatenate([cosines[:, None] * real_part - sines[:, None] * imag_part,
                            sines[:, None] * real_part + cosines[:, None] * imag_part], axis=1)


def reference(pred, target, h1, w1, w2, neighbours, rotations):
    patch_start = jnp.arange(PATCHES, dtype=jnp.int32) * R - 2 * H
    link_rows = (neighbours[:, 2 * H:2 * H + R, :] + patch_start[:, None, None]).reshape(NV, K)
    angles = rotations[:, 2 * H:2 * H + R, :].reshape(NV, K).astype(jnp.float32) * angle_step
    cosines = jnp.cos(angles)
    sine_part = jnp.sin(angles)
    values = pred.astype(jnp.float32)
    observed = target.astype(jnp.float32)

    def member_sum(member, sign_total):
        other = lax.dynamic_index_in_dim(values, member, 0, keepdims=True)
        return sign_total + jnp.sign(values - other)

    sign_total = lax.fori_loop(0, MEMBERS, member_sum, jnp.zeros(values.shape, jnp.float32))
    loss_grad = (jnp.sign(values - observed[None]) - sign_total / (MEMBERS - 1)).astype(jnp.bfloat16)

    def member_pass(pair):
        hidden, gradient = pair
        summed_rows = jnp.zeros((NV, C), jnp.float32)
        for column in range(K):
            summed_rows = summed_rows + rotate_pairs(hidden[link_rows[:, column]].astype(jnp.float32), cosines[:, column], sine_part[:, column])
        pre_act = jnp.dot(summed_rows.astype(jnp.bfloat16), w1, preferred_element_type=jnp.float32)
        grad_agg = jnp.dot(gradient, w2.T, preferred_element_type=jnp.float32)
        grad_mid = jnp.zeros((NV, C), jnp.float32)
        for column in range(K):
            grad_mid = grad_mid.at[link_rows[:, column]].add(rotate_pairs(grad_agg, cosines[:, column], -sine_part[:, column]))
        sigmoid_val = jax.nn.sigmoid(pre_act)
        act_grad = (grad_mid * sigmoid_val * (1.0 + pre_act * (1.0 - sigmoid_val))).astype(jnp.bfloat16)
        back_agg = jnp.dot(act_grad, w1.T, preferred_element_type=jnp.float32)
        spread = jnp.zeros((NV, C), jnp.float32)
        for column in range(K):
            spread = spread.at[link_rows[:, column]].add(rotate_pairs(back_agg, cosines[:, column], -sine_part[:, column]))
        return (grad_mid + spread).astype(jnp.bfloat16)

    return lax.map(member_pass, (h1, loss_grad))
```

```python
import functools

import jax
import jax.numpy as jnp
from jax import lax
from jax.experimental import pallas as pl
from jax.experimental.pallas import tpu as pltpu
from jax.sharding import PartitionSpec as P

K = 6
H = 32
MESH = pl.DeviceIdType.MESH
RELAY_SIDE = "far"


def relay_patch(side, index, half):
    if half < 32:
        return side * half + (half - 1 if side else 0)
    row = index // 2
    odd = lax.rem(index, 2)
    return side * half + 8 * row + (1 + 6 * odd if side else 6 * odd)


def relay_job(side, patch, half):
    if half < 32:
        return patch == (2 * half - 1 if side else 0), 0
    local = patch - side * half
    column = lax.rem(local, 8)
    odd, even = (7, 1) if side else (6, 0)
    mine = (local >= 0) & (local < half) & ((column == odd) | (column == even))
    return mine, 2 * (local // 8) + jnp.where(column == odd, 1, 0)


def turn_table(turns):
    diag = jnp.float32(0.70710678118654752)
    zero = jnp.zeros(turns.shape, jnp.float32)
    one = zero + 1.0

    def cosine(r):
        return jnp.where(
            r == 0,
            one,
            jnp.where(
                (r == 1) | (r == 7),
                zero + diag,
                jnp.where((r == 2) | (r == 6), zero, jnp.where(r == 4, -one, zero - diag)),
            ),
        )

    return cosine(turns), cosine((turns + 6) & 7)


def kernel(
    patches,
    members,
    pred,
    target,
    h1,
    w1,
    w2,
    links,
    turns,
    out,
    hext,
    pin,
    tin,
    gout,
    gext,
    w1v,
    w2v,
    w2c,
    maps,
    tmaps,
    deriv,
    gmid,
    back,
    relay,
    load_sem,
    pin_sem,
    tin_sem,
    pred_send,
    tgt_send,
    g_sem,
    g_send,
    h_recv,
    h_send,
    x_send,
    relay_recv,
    relay_send,
):
    me_p = lax.axis_index("patch")
    me = lax.axis_index("ens")
    half = patches // 2
    share = 256 // members
    quarter = members // 4
    pieces = members // 2
    relays = x_send.shape[0]
    row_cuts = min(4, relays)
    piece_rows, piece_cols = relay.shape
    last = patches - 1
    low, high = me < quarter, me >= members - quarter
    middle = jnp.logical_not(low | high)
    tail_side, head_side = (1, 0) if RELAY_SIDE == "far" else (0, 1)
    tail_relay, tail_index = relay_job(tail_side, me_p, half)
    head_relay, head_index = relay_job(head_side, me_p, half)

    own_h = pltpu.make_async_copy(h1, hext.at[pl.ds(64, 128)], load_sem.at[0])
    own_h.start()
    load_w2 = pltpu.make_async_copy(w2, w2v, load_sem.at[1])
    load_w2.start()
    load_w1 = pltpu.make_async_copy(w1, w1v, load_sem.at[2])
    load_w1.start()

    barrier = pltpu.get_barrier_semaphore()

    def greet(patch, ens):
        pl.semaphore_signal(
            barrier, inc=1, device_id={"patch": patch, "ens": ens}, device_id_type=MESH
        )

    def greet_own(i, carry):
        greet(me_p, lax.rem(me + i, members))
        return carry

    lax.fori_loop(1, members, greet_own, 0)

    @pl.when(low & (me_p > 0))
    def _():
        lax.fori_loop(0, members, lambda i, c: (greet(me_p - 1, i), c)[1], 0)

    @pl.when(high & (me_p < last))
    def _():
        lax.fori_loop(0, members, lambda i, c: (greet(me_p + 1, i), c)[1], 0)

    @pl.when((me_p > 0) & (me_p != half))
    def _():
        greet(me_p - 1, me)

    @pl.when((me_p < last) & (me_p != half - 1))
    def _():
        greet(me_p + 1, me)

    @pl.when(me_p == half)
    def _():
        lax.fori_loop(
            0, relays, lambda i, c: (greet(relay_patch(tail_side, i, half), me), c)[1], 0
        )

    @pl.when(me_p == half - 1)
    def _():
        lax.fori_loop(
            0, relays, lambda i, c: (greet(relay_patch(head_side, i, half), me), c)[1], 0
        )

    @pl.when(tail_relay)
    def _():
        greet(half - 1, me)

    @pl.when(head_relay)
    def _():
        greet(half, me)

    def count(flag, amount):
        return jnp.where(flag, amount, 0)

    partners = (
        (members - 1)
        + count(me_p < last, quarter)
        + count(me_p > 0, quarter)
        + count(me_p < last, count(me_p == half - 1, relays - 1) + 1)
        + count(me_p > 0, count(me_p == half, relays - 1) + 1)
        + count(tail_relay, 1)
        + count(head_relay, 1)
    )
    pl.semaphore_wait(barrier, partners)

    def send_pred(piece, patch, ens, slot):
        return pltpu.make_async_remote_copy(
            src_ref=pred.at[pl.ds(piece * share, share)],
            dst_ref=pin.at[me],
            send_sem=pred_send.at[slot],
            recv_sem=pin_sem,
            device_id={"patch": patch, "ens": ens},
            device_id_type=MESH,
        )

    own_pred = pltpu.make_async_copy(
        pred.at[pl.ds(jnp.where(middle, me - quarter, 0) * share, share)], pin.at[me], pin_sem
    )

    def each_pred(act):
        def across(i, carry):
            piece = lax.rem(me + i, pieces)
            upper = piece >= quarter

            @pl.when(upper & (me_p < last))
            def _():
                act(send_pred(piece, me_p + 1, piece - quarter, pieces + piece))

            @pl.when(jnp.logical_not(upper) & (me_p > 0))
            def _():
                act(send_pred(piece, me_p - 1, members - quarter + piece, pieces + piece))

            @pl.when(piece + quarter != me)
            def _():
                act(send_pred(piece, me_p, piece + quarter, piece))

            return carry

        lax.fori_loop(0, pieces, across, 0)

    each_pred(lambda copy: copy.start())

    def send_target(first, patch):
        return pltpu.make_async_remote_copy(
            src_ref=target.at[pl.ds(first, share)],
            dst_ref=tin,
            send_sem=tgt_send,
            recv_sem=tin_sem,
            device_id={"patch": patch, "ens": me},
            device_id_type=MESH,
        )

    def each_target(act):
        @pl.when(low & (me_p < last))
        def _():
            act(send_target((quarter + jnp.where(low, me, 0)) * share, me_p + 1))

        @pl.when(high & (me_p > 0))
        def _():
            act(send_target(jnp.where(high, me - (members - quarter), 0) * share, me_p - 1))

    each_target(lambda copy: copy.start())

    @pl.when(middle)
    def _():
        own_pred.start()
        pltpu.make_async_copy(
            target.at[pl.ds(jnp.where(middle, me - quarter, 0) * share, share)], tin, tin_sem
        ).start()

    def send_tail():
        return pltpu.make_async_remote_copy(
            src_ref=h1.at[pl.ds(64, 64)],
            dst_ref=hext.at[pl.ds(0, 64)],
            send_sem=h_send.at[0],
            recv_sem=h_recv.at[0],
            device_id={"patch": me_p + 1, "ens": me},
            device_id_type=MESH,
        )

    def send_head():
        return pltpu.make_async_remote_copy(
            src_ref=h1.at[pl.ds(0, 64)],
            dst_ref=hext.at[pl.ds(192, 64)],
            send_sem=h_send.at[1],
            recv_sem=h_recv.at[1],
            device_id={"patch": me_p - 1, "ens": me},
            device_id_type=MESH,
        )

    def cut(ref, index, first):
        row = lax.rem(index, row_cuts) * piece_rows + first
        column = pl.multiple_of((index // row_cuts) * piece_cols, 128)
        return ref.at[pl.ds(pl.multiple_of(row, 16), piece_rows), pl.ds(column, piece_cols)]

    def to_relay(index, first, side):
        return pltpu.make_async_remote_copy(
            src_ref=cut(h1, index, first),
            dst_ref=relay,
            send_sem=x_send.at[index],
            recv_sem=relay_recv,
            device_id={"patch": relay_patch(side, index, half), "ens": me},
            device_id_type=MESH,
        )

    def each_halo(act):
        @pl.when((me_p < last) & (me_p != half - 1))
        def _():
            act(send_tail())

        @pl.when((me_p > 0) & (me_p != half))
        def _():
            act(send_head())

        @pl.when(me_p == half - 1)
        def _():
            lax.fori_loop(0, relays, lambda i, c: (act(to_relay(i, 64, tail_side)), c)[1], 0)

        @pl.when(me_p == half)
        def _():
            lax.fori_loop(0, relays, lambda i, c: (act(to_relay(i, 0, head_side)), c)[1], 0)

    each_halo(lambda copy: copy.start())

    def onward(index, first, patch, slot):
        return pltpu.make_async_remote_copy(
            src_ref=relay,
            dst_ref=cut(hext, index, first),
            send_sem=relay_send,
            recv_sem=h_recv.at[slot],
            device_id={"patch": patch, "ens": me},
            device_id_type=MESH,
        )

    def each_relay(act):
        @pl.when(tail_relay)
        def _():
            act(onward(jnp.where(tail_relay, tail_index, 0), 0, half, 0))

        @pl.when(head_relay)
        def _():
            act(onward(jnp.where(head_relay, head_index, 0), 192, half - 1, 1))

    for first in range(0, 256, 128):
        rows = slice(first, first + 128)
        slots = lax.broadcasted_iota(jnp.int32, (128, 256), 0) + first
        cos_map = jnp.zeros((128, 256), jnp.float32)
        sin_map = jnp.zeros((128, 256), jnp.float32)
        for column in range(K):
            cosine, sine = turn_table(turns[column])
            hit = links[column] == slots
            cos_map += jnp.where(hit, cosine, 0.0)
            sin_map += jnp.where(hit, sine, 0.0)
        tmaps[0, rows] = cos_map.astype(jnp.bfloat16)
        tmaps[1, rows] = sin_map.astype(jnp.bfloat16)
        maps[0, :, rows] = cos_map.T.astype(jnp.bfloat16)
        maps[1, :, rows] = sin_map.T.astype(jnp.bfloat16)

    @pl.when(me_p == 0)
    def _():
        hext[0:64] = jnp.zeros((64, hext.shape[1]), hext.dtype)

    @pl.when(me_p == last)
    def _():
        hext[192:256] = jnp.zeros((64, hext.shape[1]), hext.dtype)

    @pl.when(tail_relay | head_relay)
    def _():
        pltpu.make_async_copy(relay, relay, relay_recv).wait()

    each_relay(lambda copy: copy.start())

    outside = (low & (me_p == 0)) | (high & (me_p == last))

    @pl.when(outside)
    def _():
        pin[...] = jnp.zeros(pin.shape, pin.dtype)
        tin[...] = jnp.zeros(tin.shape, tin.dtype)

    @pl.when(jnp.logical_not(outside))
    def _():
        pltpu.make_async_copy(pin, pin, pin_sem).wait()
        pltpu.make_async_copy(tin, tin, tin_sem).wait()

    def side_of(left, right):
        return jnp.where(left > right, 1.0, jnp.where(left < right, -1.0, 0.0))

    values = pin[...].astype(jnp.float32)
    observed = tin[...].astype(jnp.float32)
    total = jnp.zeros(values.shape, jnp.float32)
    for shift in range(1, members // 2 + 1):
        other = jnp.concatenate([values[shift:], values[:shift]], axis=0)
        side = side_of(values, other)
        total += side
        if shift < members // 2:
            total -= jnp.concatenate([side[members - shift :], side[: members - shift]], axis=0)
    gout[...] = (side_of(values, observed[None]) - total / (members - 1)).astype(jnp.bfloat16)

    def send_grad(i):
        to = lax.rem(me + i, members)
        return pltpu.make_async_remote_copy(
            src_ref=gout.at[to],
            dst_ref=gext.at[me],
            send_sem=g_send.at[i],
            recv_sem=g_sem,
            device_id={"patch": me_p, "ens": to},
            device_id_type=MESH,
        )

    lax.fori_loop(1, members, lambda i, c: (send_grad(i).start(), c)[1], 0)
    pltpu.make_async_copy(gout.at[me], gext.at[me], g_sem).start()

    load_w2.wait()
    w2c[0:512, 0:128] = w2v[0:512]
    w2c[0:512, 128:256] = w2v[512:1024]
    w2c[512:1024, 0:128] = w2v[512:1024]
    w2c[512:1024, 128:256] = -w2v[0:512]

    own_h.wait()

    @pl.when(me_p > 0)
    def _():
        pltpu.make_async_copy(hext.at[pl.ds(0, 64)], hext.at[pl.ds(0, 64)], h_recv.at[0]).wait()

    @pl.when(me_p < last)
    def _():
        pltpu.make_async_copy(
            hext.at[pl.ds(192, 64)], hext.at[pl.ds(192, 64)], h_recv.at[1]
        ).wait()

    features = hext[...]
    by_cos = jnp.dot(maps[0, 32:224], features, preferred_element_type=jnp.float32)
    by_sin = jnp.dot(maps[1, 32:224], features, preferred_element_type=jnp.float32)
    summed = jnp.concatenate(
        [
            (by_cos[:, :512] - by_sin[:, 512:]).astype(jnp.bfloat16),
            (by_sin[:, :512] + by_cos[:, 512:]).astype(jnp.bfloat16),
        ],
        axis=1,
    )
    load_w1.wait()
    pre_act = jnp.dot(summed, w1v[...], preferred_element_type=jnp.float32)
    sigmoid = jax.nn.sigmoid(pre_act)
    deriv[...] = sigmoid * (1.0 + pre_act * (1.0 - sigmoid))
    back[0:32] = jnp.zeros((32, back.shape[1]), back.dtype)
    back[224:256] = jnp.zeros((32, back.shape[1]), back.dtype)

    pltpu.make_async_copy(gext, gext, g_sem).wait()
    grads = gext[...].reshape(256, 128)
    spread_grads = jnp.concatenate(
        [
            jnp.dot(tmaps[0, 32:224], grads, preferred_element_type=jnp.float32),
            jnp.dot(tmaps[1, 32:224], grads, preferred_element_type=jnp.float32),
        ],
        axis=1,
    ).astype(jnp.bfloat16)
    contract_last = (((1,), (1,)), ((), ()))
    gmid[...] = lax.dot_general(
        spread_grads, w2c[...], contract_last, preferred_element_type=jnp.float32
    )
    act_grad = (gmid[...] * deriv[...]).astype(jnp.bfloat16)
    back[32:224] = lax.dot_general(
        act_grad, w1v[...], contract_last, preferred_element_type=jnp.float32
    ).astype(jnp.bfloat16)
    rows_back = back[...]
    by_cos = jnp.dot(tmaps[0, 64:192], rows_back, preferred_element_type=jnp.float32)
    by_sin = jnp.dot(tmaps[1, 64:192], rows_back, preferred_element_type=jnp.float32)
    out[:, :512] = (gmid[32:160, :512] + by_cos[:, :512] + by_sin[:, 512:]).astype(out.dtype)
    out[:, 512:] = (gmid[32:160, 512:] + by_cos[:, 512:] - by_sin[:, :512]).astype(out.dtype)

    each_pred(lambda copy: copy.wait_send())
    each_target(lambda copy: copy.wait_send())
    each_halo(lambda copy: copy.wait_send())
    each_relay(lambda copy: copy.wait_send())
    lax.fori_loop(1, members, lambda i, c: (send_grad(i).wait_send(), c)[1], 0)


def per_device(pred, target, h1, w1, w2, neighbours, rotations):
    members = lax.axis_size("ens")
    patches = lax.axis_size("patch")
    rows, channels = h1.shape[1:]
    share = 256 // members
    relays = 8 if patches >= 64 else 1
    row_cuts = min(4, relays)
    anywhere = pl.BlockSpec(memory_space=pltpu.HBM)
    vmem = pl.BlockSpec(memory_space=pltpu.VMEM)
    dma = pltpu.SemaphoreType.DMA
    bf16 = jnp.bfloat16
    result = pl.pallas_call(
        functools.partial(kernel, patches, members),
        out_shape=jax.ShapeDtypeStruct((rows, channels), bf16),
        in_specs=[anywhere, anywhere, anywhere, anywhere, anywhere, vmem, vmem],
        out_specs=vmem,
        scratch_shapes=[
            pltpu.VMEM((256, channels), bf16),
            pltpu.VMEM((members, share, 128), bf16),
            pltpu.VMEM((share, 128), bf16),
            pltpu.VMEM((members, share, 128), bf16),
            pltpu.VMEM((members, share, 128), bf16),
            pltpu.VMEM((channels, channels), bf16),
            pltpu.VMEM((channels, 128), bf16),
            pltpu.VMEM((channels, 256), bf16),
            pltpu.VMEM((2, 256, 256), bf16),
            pltpu.VMEM((2, 256, 256), bf16),
            pltpu.VMEM((192, channels), jnp.float32),
            pltpu.VMEM((192, channels), jnp.float32),
            pltpu.VMEM((256, channels), bf16),
            pltpu.VMEM((64 // row_cuts, channels * row_cuts // relays), bf16),
            dma((3,)),
            dma(()),
            dma(()),
            dma((members,)),
            dma(()),
            dma(()),
            dma((members,)),
            dma((2,)),
            dma((2,)),
            dma((relays,)),
            dma(()),
            dma(()),
        ],
        compiler_params=pltpu.CompilerParams(
            collective_id=0, has_side_effects=True, vmem_limit_bytes=62 * 2**20
        ),
        name="mesh_backward",
    )(
        pred[0],
        target,
        h1[0],
        w1,
        w2,
        jnp.transpose(neighbours, (2, 0, 1)),
        jnp.transpose(rotations, (2, 0, 1)),
    )
    return result[None]


def solution(mesh):
    return jax.shard_map(
        per_device,
        mesh=mesh,
        in_specs=(
            P("ens", "patch", None),
            P("patch", None),
            P("ens", "patch", None),
            P(),
            P(),
            P("patch", None, None),
            P("patch", None, None),
        ),
        out_specs=P("ens", "patch", None),
        check_vma=False,
    )
```

```python
import functools

import jax
import jax.numpy as jnp
from jax import lax
from jax.experimental import pallas as pl
from jax.experimental.pallas import tpu as pltpu
from jax.sharding import PartitionSpec as P

K = 6
H = 32
MESH = pl.DeviceIdType.MESH
RELAY_SIDE = "near"


def relay_patch(side, index, half):
    if half < 32:
        return side * half + (half - 1 if side else 0)
    row = index // 2
    odd = lax.rem(index, 2)
    return side * half + 8 * row + (2 + 5 * odd if side else 1 + 5 * odd)


def relay_job(side, patch, half):
    if half < 32:
        return patch == (2 * half - 1 if side else 0), 0
    local = patch - side * half
    column = lax.rem(local, 8)
    odd, even = (7, 2) if side else (6, 1)
    mine = (local >= 0) & (local < half) & ((column == odd) | (column == even))
    return mine, 2 * (local // 8) + jnp.where(column == odd, 1, 0)


def turn_table(turns):
    diag = jnp.float32(0.70710678118654752)
    zero = jnp.zeros(turns.shape, jnp.float32)
    one = zero + 1.0

    def cosine(r):
        return jnp.where(
            r == 0,
            one,
            jnp.where(
                (r == 1) | (r == 7),
                zero + diag,
                jnp.where((r == 2) | (r == 6), zero, jnp.where(r == 4, -one, zero - diag)),
            ),
        )

    return cosine(turns), cosine((turns + 6) & 7)


def kernel(
    patches,
    members,
    pred,
    target,
    h1,
    w1,
    w2,
    links,
    turns,
    out,
    hext,
    pin,
    tin,
    gout,
    gext,
    w1v,
    w2v,
    w2c,
    maps,
    tmaps,
    deriv,
    gmid,
    back,
    relay,
    load_sem,
    pin_sem,
    tin_sem,
    pred_send,
    tgt_send,
    g_sem,
    g_send,
    h_recv,
    h_send,
    x_send,
    relay_recv,
    relay_send,
    ready,
):
    me_p = lax.axis_index("patch")
    me = lax.axis_index("ens")
    half = patches // 2
    scorers = members // 2
    share = 256 // scorers
    pieces = scorers // 2
    quarter = scorers // 4
    base = members // 4
    relays = x_send.shape[0]
    row_cuts = min(4, relays)
    piece_rows, piece_cols = relay.shape
    last = patches - 1
    place = me - base
    scorer = (place >= 0) & (place < scorers)
    low = scorer & (place < quarter)
    high = scorer & (place >= scorers - quarter)
    middle = (place >= quarter) & (place < scorers - quarter)
    tail_side, head_side = (1, 0) if RELAY_SIDE == "far" else (0, 1)
    tail_relay, tail_index = relay_job(tail_side, me_p, half)
    head_relay, head_index = relay_job(head_side, me_p, half)

    own_h = pltpu.make_async_copy(h1, hext.at[pl.ds(64, 128)], load_sem.at[0])
    own_h.start()
    load_w2 = pltpu.make_async_copy(w2, w2v, load_sem.at[1])
    load_w2.start()
    load_w1 = pltpu.make_async_copy(w1, w1v, load_sem.at[2])
    load_w1.start()

    barrier = pltpu.get_barrier_semaphore()

    def greet(patch, ens):
        pl.semaphore_signal(
            barrier, inc=1, device_id={"patch": patch, "ens": ens}, device_id_type=MESH
        )

    def greet_own(i, carry):
        greet(me_p, lax.rem(me + i, members))
        return carry

    @pl.when(scorer)
    def _():
        lax.fori_loop(1, members, greet_own, 0)

    @pl.when(low & (me_p > 0))
    def _():
        lax.fori_loop(0, members, lambda i, c: (greet(me_p - 1, i), c)[1], 0)

    @pl.when(high & (me_p < last))
    def _():
        lax.fori_loop(0, members, lambda i, c: (greet(me_p + 1, i), c)[1], 0)

    @pl.when((me_p > 0) & (me_p != half))
    def _():
        greet(me_p - 1, me)

    @pl.when((me_p < last) & (me_p != half - 1))
    def _():
        greet(me_p + 1, me)

    @pl.when(me_p == half)
    def _():
        lax.fori_loop(
            0, relays, lambda i, c: (greet(relay_patch(tail_side, i, half), me), c)[1], 0
        )

    @pl.when(me_p == half - 1)
    def _():
        lax.fori_loop(
            0, relays, lambda i, c: (greet(relay_patch(head_side, i, half), me), c)[1], 0
        )

    @pl.when(tail_relay)
    def _():
        greet(half - 1, me)

    @pl.when(head_relay)
    def _():
        greet(half, me)

    def count(flag, amount):
        return jnp.where(flag, amount, 0)

    partners = (
        scorers
        - count(scorer, 1)
        + count(me_p < last, quarter)
        + count(me_p > 0, quarter)
        + count(me_p < last, count(me_p == half - 1, relays - 1) + 1)
        + count(me_p > 0, count(me_p == half, relays - 1) + 1)
        + count(tail_relay, 1)
        + count(head_relay, 1)
    )
    pl.semaphore_wait(barrier, partners)

    def tell(i, carry):
        @pl.when(i != place)
        def _():
            pl.semaphore_signal(
                ready, inc=1, device_id={"patch": me_p, "ens": base + i}, device_id_type=MESH
            )

        return carry

    lax.fori_loop(0, scorers, tell, 0)

    def send_pred(piece, patch, to, slot):
        return pltpu.make_async_remote_copy(
            src_ref=pred.at[pl.ds(pl.multiple_of(piece * share, 16), share)],
            dst_ref=pin.at[me],
            send_sem=pred_send.at[slot],
            recv_sem=pin_sem,
            device_id={"patch": patch, "ens": base + to},
            device_id_type=MESH,
        )

    def each_pred(act):
        def across(i, carry):
            piece = lax.rem(me + i, pieces)
            upper = piece >= quarter

            @pl.when(upper & (me_p < last))
            def _():
                act(send_pred(piece, me_p + 1, piece - quarter, pieces + piece))

            @pl.when(jnp.logical_not(upper) & (me_p > 0))
            def _():
                act(send_pred(piece, me_p - 1, scorers - quarter + piece, pieces + piece))

            @pl.when(piece + quarter != place)
            def _():
                act(send_pred(piece, me_p, piece + quarter, piece))

            return carry

        lax.fori_loop(0, pieces, across, 0)

    each_pred(lambda copy: copy.start())

    def send_target(first, patch):
        return pltpu.make_async_remote_copy(
            src_ref=target.at[pl.ds(pl.multiple_of(first, 16), share)],
            dst_ref=tin,
            send_sem=tgt_send,
            recv_sem=tin_sem,
            device_id={"patch": patch, "ens": me},
            device_id_type=MESH,
        )

    def each_target(act):
        @pl.when(low & (me_p < last))
        def _():
            act(send_target((quarter + jnp.where(low, place, 0)) * share, me_p + 1))

        @pl.when(high & (me_p > 0))
        def _():
            act(send_target(jnp.where(high, place - (scorers - quarter), 0) * share, me_p - 1))

    each_target(lambda copy: copy.start())

    @pl.when(middle)
    def _():
        own = pl.ds(pl.multiple_of(jnp.where(middle, place - quarter, 0) * share, 16), share)
        pltpu.make_async_copy(pred.at[own], pin.at[me], pin_sem).start()
        pltpu.make_async_copy(target.at[own], tin, tin_sem).start()

    def send_tail():
        return pltpu.make_async_remote_copy(
            src_ref=h1.at[pl.ds(64, 64)],
            dst_ref=hext.at[pl.ds(0, 64)],
            send_sem=h_send.at[0],
            recv_sem=h_recv.at[0],
            device_id={"patch": me_p + 1, "ens": me},
            device_id_type=MESH,
        )

    def send_head():
        return pltpu.make_async_remote_copy(
            src_ref=h1.at[pl.ds(0, 64)],
            dst_ref=hext.at[pl.ds(192, 64)],
            send_sem=h_send.at[1],
            recv_sem=h_recv.at[1],
            device_id={"patch": me_p - 1, "ens": me},
            device_id_type=MESH,
        )

    def cut(ref, index, first):
        row = lax.rem(index, row_cuts) * piece_rows + first
        column = pl.multiple_of((index // row_cuts) * piece_cols, 128)
        return ref.at[pl.ds(pl.multiple_of(row, 16), piece_rows), pl.ds(column, piece_cols)]

    def to_relay(index, first, side):
        return pltpu.make_async_remote_copy(
            src_ref=cut(h1, index, first),
            dst_ref=relay,
            send_sem=x_send.at[index],
            recv_sem=relay_recv,
            device_id={"patch": relay_patch(side, index, half), "ens": me},
            device_id_type=MESH,
        )

    def each_halo(act):
        @pl.when((me_p < last) & (me_p != half - 1))
        def _():
            act(send_tail())

        @pl.when((me_p > 0) & (me_p != half))
        def _():
            act(send_head())

        @pl.when(me_p == half - 1)
        def _():
            lax.fori_loop(0, relays, lambda i, c: (act(to_relay(i, 64, tail_side)), c)[1], 0)

        @pl.when(me_p == half)
        def _():
            lax.fori_loop(0, relays, lambda i, c: (act(to_relay(i, 0, head_side)), c)[1], 0)

    each_halo(lambda copy: copy.start())

    def onward(index, first, patch, slot):
        return pltpu.make_async_remote_copy(
            src_ref=relay,
            dst_ref=cut(hext, index, first),
            send_sem=relay_send,
            recv_sem=h_recv.at[slot],
            device_id={"patch": patch, "ens": me},
            device_id_type=MESH,
        )

    def each_relay(act):
        @pl.when(tail_relay)
        def _():
            act(onward(jnp.where(tail_relay, tail_index, 0), 0, half, 0))

        @pl.when(head_relay)
        def _():
            act(onward(jnp.where(head_relay, head_index, 0), 192, half - 1, 1))

    for first in range(0, 256, 128):
        rows = slice(first, first + 128)
        slots = lax.broadcasted_iota(jnp.int32, (128, 256), 0) + first
        cos_map = jnp.zeros((128, 256), jnp.float32)
        sin_map = jnp.zeros((128, 256), jnp.float32)
        for column in range(K):
            cosine, sine = turn_table(turns[column])
            hit = links[column] == slots
            cos_map += jnp.where(hit, cosine, 0.0)
            sin_map += jnp.where(hit, sine, 0.0)
        tmaps[0, rows] = cos_map.astype(jnp.bfloat16)
        tmaps[1, rows] = sin_map.astype(jnp.bfloat16)
        maps[0, :, rows] = cos_map.T.astype(jnp.bfloat16)
        maps[1, :, rows] = sin_map.T.astype(jnp.bfloat16)

    @pl.when(me_p == 0)
    def _():
        hext[0:64] = jnp.zeros((64, hext.shape[1]), hext.dtype)

    @pl.when(me_p == last)
    def _():
        hext[192:256] = jnp.zeros((64, hext.shape[1]), hext.dtype)

    @pl.when(tail_relay | head_relay)
    def _():
        pltpu.make_async_copy(relay, relay, relay_recv).wait()

    each_relay(lambda copy: copy.start())

    outside = (low & (me_p == 0)) | (high & (me_p == last))

    def side_of(left, right):
        return jnp.where(left > right, 1.0, jnp.where(left < right, -1.0, 0.0))

    def send_grad(i):
        to = lax.rem(me + i, members)
        return pltpu.make_async_remote_copy(
            src_ref=gout.at[to],
            dst_ref=gext.at[jnp.where(scorer, place, 0)],
            send_sem=g_send.at[i],
            recv_sem=g_sem,
            device_id={"patch": me_p, "ens": to},
            device_id_type=MESH,
        )

    @pl.when(scorer)
    def _():
        @pl.when(outside)
        def _():
            pin[...] = jnp.zeros(pin.shape, pin.dtype)
            tin[...] = jnp.zeros(tin.shape, tin.dtype)

        @pl.when(jnp.logical_not(outside))
        def _():
            with jax.named_scope("wait_pred"):
                pltpu.make_async_copy(pin, pin, pin_sem).wait()
                pltpu.make_async_copy(tin, tin, tin_sem).wait()

        with jax.named_scope("score"):
            for first in range(0, share, 16):
                rows = slice(first, first + 16)
                values = pin[:, rows].astype(jnp.float32)
                observed = tin[rows].astype(jnp.float32)
                total = jnp.zeros(values.shape, jnp.float32)
                for shift in range(1, members // 2 + 1):
                    other = jnp.concatenate([values[shift:], values[:shift]], axis=0)
                    side = side_of(values, other)
                    total += side
                    if shift < members // 2:
                        total -= jnp.concatenate(
                            [side[members - shift :], side[: members - shift]], axis=0
                        )
                own_side = side_of(values, observed[None])
                gout[:, rows] = (own_side - total / (members - 1)).astype(jnp.bfloat16)
        with jax.named_scope("send_grad"):
            pl.semaphore_wait(ready, members - 1)
            lax.fori_loop(1, members, lambda i, c: (send_grad(i).start(), c)[1], 0)
            pltpu.make_async_copy(
                gout.at[me], gext.at[jnp.where(scorer, place, 0)], g_sem
            ).start()

    load_w2.wait()
    w2c[0:512, 0:128] = w2v[0:512]
    w2c[0:512, 128:256] = w2v[512:1024]
    w2c[512:1024, 0:128] = w2v[512:1024]
    w2c[512:1024, 128:256] = -w2v[0:512]

    own_h.wait()

    @pl.when(me_p > 0)
    def _():
        pltpu.make_async_copy(hext.at[pl.ds(0, 64)], hext.at[pl.ds(0, 64)], h_recv.at[0]).wait()

    @pl.when(me_p < last)
    def _():
        pltpu.make_async_copy(
            hext.at[pl.ds(192, 64)], hext.at[pl.ds(192, 64)], h_recv.at[1]
        ).wait()

    features = hext[...]
    by_cos = jnp.dot(maps[0, 32:224], features, preferred_element_type=jnp.float32)
    by_sin = jnp.dot(maps[1, 32:224], features, preferred_element_type=jnp.float32)
    summed = jnp.concatenate(
        [
            (by_cos[:, :512] - by_sin[:, 512:]).astype(jnp.bfloat16),
            (by_sin[:, :512] + by_cos[:, 512:]).astype(jnp.bfloat16),
        ],
        axis=1,
    )
    load_w1.wait()
    pre_act = jnp.dot(summed, w1v[...], preferred_element_type=jnp.float32)
    sigmoid = jax.nn.sigmoid(pre_act)
    deriv[...] = sigmoid * (1.0 + pre_act * (1.0 - sigmoid))
    back[0:32] = jnp.zeros((32, back.shape[1]), back.dtype)
    back[224:256] = jnp.zeros((32, back.shape[1]), back.dtype)

    pltpu.make_async_copy(gext, gext, g_sem).wait()
    grads = gext[...].reshape(256, 128)
    spread_grads = jnp.concatenate(
        [
            jnp.dot(tmaps[0, 32:224], grads, preferred_element_type=jnp.float32),
            jnp.dot(tmaps[1, 32:224], grads, preferred_element_type=jnp.float32),
        ],
        axis=1,
    ).astype(jnp.bfloat16)
    contract_last = (((1,), (1,)), ((), ()))
    gmid[...] = lax.dot_general(
        spread_grads, w2c[...], contract_last, preferred_element_type=jnp.float32
    )
    act_grad = (gmid[...] * deriv[...]).astype(jnp.bfloat16)
    back[32:224] = lax.dot_general(
        act_grad, w1v[...], contract_last, preferred_element_type=jnp.float32
    ).astype(jnp.bfloat16)
    rows_back = back[...]
    by_cos = jnp.dot(tmaps[0, 64:192], rows_back, preferred_element_type=jnp.float32)
    by_sin = jnp.dot(tmaps[1, 64:192], rows_back, preferred_element_type=jnp.float32)
    out[:, :512] = (gmid[32:160, :512] + by_cos[:, :512] + by_sin[:, 512:]).astype(out.dtype)
    out[:, 512:] = (gmid[32:160, 512:] + by_cos[:, 512:] - by_sin[:, :512]).astype(out.dtype)

    each_pred(lambda copy: copy.wait_send())
    each_target(lambda copy: copy.wait_send())
    each_halo(lambda copy: copy.wait_send())
    each_relay(lambda copy: copy.wait_send())

    @pl.when(scorer)
    def _():
        lax.fori_loop(1, members, lambda i, c: (send_grad(i).wait_send(), c)[1], 0)


def per_device(pred, target, h1, w1, w2, neighbours, rotations):
    members = lax.axis_size("ens")
    patches = lax.axis_size("patch")
    rows, channels = h1.shape[1:]
    scorers = members // 2
    share = 256 // scorers
    relays = 8 if patches >= 64 else 1
    row_cuts = min(4, relays)
    anywhere = pl.BlockSpec(memory_space=pltpu.HBM)
    vmem = pl.BlockSpec(memory_space=pltpu.VMEM)
    dma = pltpu.SemaphoreType.DMA
    bf16 = jnp.bfloat16
    result = pl.pallas_call(
        functools.partial(kernel, patches, members),
        out_shape=jax.ShapeDtypeStruct((rows, channels), bf16),
        in_specs=[anywhere, anywhere, anywhere, anywhere, anywhere, vmem, vmem],
        out_specs=vmem,
        scratch_shapes=[
            pltpu.VMEM((256, channels), bf16),
            pltpu.VMEM((members, share, 128), bf16),
            pltpu.VMEM((share, 128), bf16),
            pltpu.VMEM((members, share, 128), bf16),
            pltpu.VMEM((scorers, share, 128), bf16),
            pltpu.VMEM((channels, channels), bf16),
            pltpu.VMEM((channels, 128), bf16),
            pltpu.VMEM((channels, 256), bf16),
            pltpu.VMEM((2, 256, 256), bf16),
            pltpu.VMEM((2, 256, 256), bf16),
            pltpu.VMEM((192, channels), jnp.float32),
            pltpu.VMEM((192, channels), jnp.float32),
            pltpu.VMEM((256, channels), bf16),
            pltpu.VMEM((64 // row_cuts, channels * row_cuts // relays), bf16),
            dma((3,)),
            dma(()),
            dma(()),
            dma((members,)),
            dma(()),
            dma(()),
            dma((members,)),
            dma((2,)),
            dma((2,)),
            dma((relays,)),
            dma(()),
            dma(()),
            pltpu.SemaphoreType.REGULAR,
        ],
        compiler_params=pltpu.CompilerParams(
            collective_id=0, has_side_effects=True, vmem_limit_bytes=62 * 2**20
        ),
        name="mesh_backward",
    )(
        pred[0],
        target,
        h1[0],
        w1,
        w2,
        jnp.transpose(neighbours, (2, 0, 1)),
        jnp.transpose(rotations, (2, 0, 1)),
    )
    return result[None]


def solution(mesh):
    return jax.shard_map(
        per_device,
        mesh=mesh,
        in_specs=(
            P("ens", "patch", None),
            P("patch", None),
            P("ens", "patch", None),
            P(),
            P(),
            P("patch", None, None),
            P("patch", None, None),
        ),
        out_specs=P("ens", "patch", None),
        check_vma=False,
    )
```

```python
import functools

import jax
import jax.numpy as jnp
from jax import lax
from jax.experimental import pallas as pl
from jax.experimental.pallas import tpu as pltpu
from jax.sharding import PartitionSpec as P

K = 6
H = 32
MESH = pl.DeviceIdType.MESH


def relay_patches(side, half):
    if half < 32:
        return (half - 1 + half,) if side else (0,)
    return (40, 63, 56, 39) if side else (23, 24, 7, 0)


def relay_patch(side, index, half):
    patches = relay_patches(side, half)
    patch = jnp.int32(patches[0])
    for i, other in enumerate(patches):
        patch = jnp.where(index == i, other, patch)
    return patch


def relay_job(side, patch, half):
    mine, index = patch < 0, jnp.int32(0)
    for i, other in enumerate(relay_patches(side, half)):
        mine = mine | (patch == other)
        index = jnp.where(patch == other, i, index)
    return mine, index


def turn_table(turns):
    diag = jnp.float32(0.70710678118654752)
    zero = jnp.zeros(turns.shape, jnp.float32)
    one = zero + 1.0

    def cosine(r):
        return jnp.where(
            r == 0,
            one,
            jnp.where(
                (r == 1) | (r == 7),
                zero + diag,
                jnp.where((r == 2) | (r == 6), zero, jnp.where(r == 4, -one, zero - diag)),
            ),
        )

    return cosine(turns), cosine((turns + 6) & 7)


def kernel(
    patches,
    members,
    pred,
    target,
    h1,
    w1,
    w2,
    links,
    turns,
    out,
    hext,
    pin,
    tin,
    gout,
    gext,
    w1v,
    w2v,
    w2c,
    maps,
    tmaps,
    deriv,
    gmid,
    back,
    relay,
    load_sem,
    pin_sem,
    tin_sem,
    pred_send,
    tgt_send,
    g_sem,
    g_send,
    h_recv,
    h_send,
    x_send,
    relay_recv,
    relay_send,
    ready,
    cross,
    c_send,
):
    me_p = lax.axis_index("patch")
    me = lax.axis_index("ens")
    half = patches // 2
    scorers = members // 2
    share = 256 // scorers
    pieces = scorers // 2
    quarter = scorers // 4
    base = members // 4
    relays = x_send.shape[0]
    row_cuts = min(4, relays)
    piece_rows, piece_cols = relay.shape
    last = patches - 1
    place = me - base
    scorer = (place >= 0) & (place < scorers)
    low = scorer & (place < quarter)
    high = scorer & (place >= scorers - quarter)
    middle = (place >= quarter) & (place < scorers - quarter)
    tail_side, head_side = 0, 1
    under, over = me_p == half - 1, me_p == half
    has_left = (me_p > 0) & jnp.logical_not(over)
    has_right = (me_p < last) & jnp.logical_not(under)
    tail_scorer = under & middle & (place >= pieces)
    head_scorer = over & middle & (place < pieces)
    tail_relay, tail_index = relay_job(tail_side, me_p, half)
    head_relay, head_index = relay_job(head_side, me_p, half)

    own_h = pltpu.make_async_copy(h1, hext.at[pl.ds(64, 128)], load_sem.at[0])
    own_h.start()
    load_w2 = pltpu.make_async_copy(w2, w2v, load_sem.at[1])
    load_w2.start()
    load_w1 = pltpu.make_async_copy(w1, w1v, load_sem.at[2])
    load_w1.start()

    barrier = pltpu.get_barrier_semaphore()

    def greet(patch, ens):
        pl.semaphore_signal(
            barrier, inc=1, device_id={"patch": patch, "ens": ens}, device_id_type=MESH
        )

    def greet_own(i, carry):
        greet(me_p, lax.rem(me + i, members))
        return carry

    @pl.when(scorer)
    def _():
        lax.fori_loop(1, members, greet_own, 0)

    @pl.when(low & has_left)
    def _():
        lax.fori_loop(0, members, lambda i, c: (greet(me_p - 1, i), c)[1], 0)

    @pl.when(high & has_right)
    def _():
        lax.fori_loop(0, members, lambda i, c: (greet(me_p + 1, i), c)[1], 0)

    @pl.when(has_left)
    def _():
        greet(me_p - 1, me)

    @pl.when(has_right)
    def _():
        greet(me_p + 1, me)

    @pl.when(under)
    def _():
        lax.fori_loop(
            0, relays, lambda i, c: (greet(relay_patch(head_side, i, half), me), c)[1], 0
        )
        lax.fori_loop(quarter, pieces, lambda i, c: (greet(half, base + i), c)[1], 0)

    @pl.when(tail_scorer)
    def _():
        lax.fori_loop(0, members, lambda i, c: (greet(half, i), c)[1], 0)

    @pl.when(tail_relay)
    def _():
        greet(half - 1, me)
        greet(half, me)

    @pl.when(head_relay)
    def _():
        greet(half, me)

    def count(flag, amount):
        return jnp.where(flag, amount, 0)

    partners = (
        scorers
        - count(scorer, 1)
        + count(has_right, quarter)
        + count(has_left, quarter)
        + count(me_p < last, count(me_p == half - 1, relays - 1) + 1)
        + count(me_p > 0, count(me_p == half, relays - 1) + 1)
        + count(over, relays + quarter)
        + count(head_scorer, members)
        + count(head_relay, 1)
    )
    pl.semaphore_wait(barrier, partners)

    def tell(i, carry):
        @pl.when(i != place)
        def _():
            pl.semaphore_signal(
                ready, inc=1, device_id={"patch": me_p, "ens": base + i}, device_id_type=MESH
            )

        return carry

    lax.fori_loop(0, scorers, tell, 0)

    def tell_across(patch, ens):
        pl.semaphore_signal(
            cross, inc=1, device_id={"patch": patch, "ens": ens}, device_id_type=MESH
        )

    @pl.when(over)
    def _():
        lax.fori_loop(
            0, relays, lambda i, c: (tell_across(relay_patch(tail_side, i, half), me), c)[1], 0
        )
        lax.fori_loop(
            pieces, pieces + quarter, lambda i, c: (tell_across(half - 1, base + i), c)[1], 0
        )

    def send_pred(piece, patch, to, slot):
        return pltpu.make_async_remote_copy(
            src_ref=pred.at[pl.ds(pl.multiple_of(piece * share, 16), share)],
            dst_ref=pin.at[me],
            send_sem=pred_send.at[slot],
            recv_sem=pin_sem,
            device_id={"patch": patch, "ens": base + to},
            device_id_type=MESH,
        )

    def each_pred(act):
        def across(i, carry):
            piece = lax.rem(me + i, pieces)
            upper = piece >= quarter

            @pl.when(upper & has_right)
            def _():
                act(send_pred(piece, me_p + 1, piece - quarter, pieces + piece))

            @pl.when(jnp.logical_not(upper) & has_left)
            def _():
                act(send_pred(piece, me_p - 1, scorers - quarter + piece, pieces + piece))

            @pl.when(piece + quarter != place)
            def _():
                act(send_pred(piece, me_p, piece + quarter, piece))

            return carry

        lax.fori_loop(0, pieces, across, 0)

    each_pred(lambda copy: copy.start())

    def send_target(first, patch):
        return pltpu.make_async_remote_copy(
            src_ref=target.at[pl.ds(pl.multiple_of(first, 16), share)],
            dst_ref=tin,
            send_sem=tgt_send,
            recv_sem=tin_sem,
            device_id={"patch": patch, "ens": me},
            device_id_type=MESH,
        )

    def each_target(act):
        @pl.when(low & has_right)
        def _():
            act(send_target((quarter + jnp.where(low, place, 0)) * share, me_p + 1))

        @pl.when(high & has_left)
        def _():
            act(send_target(jnp.where(high, place - (scorers - quarter), 0) * share, me_p - 1))

    each_target(lambda copy: copy.start())

    @pl.when(middle)
    def _():
        own = pl.ds(pl.multiple_of(jnp.where(middle, place - quarter, 0) * share, 16), share)
        pltpu.make_async_copy(pred.at[own], pin.at[me], pin_sem).start()
        pltpu.make_async_copy(target.at[own], tin, tin_sem).start()

    def send_tail():
        return pltpu.make_async_remote_copy(
            src_ref=h1.at[pl.ds(64, 64)],
            dst_ref=hext.at[pl.ds(0, 64)],
            send_sem=h_send.at[0],
            recv_sem=h_recv.at[0],
            device_id={"patch": me_p + 1, "ens": me},
            device_id_type=MESH,
        )

    def send_head():
        return pltpu.make_async_remote_copy(
            src_ref=h1.at[pl.ds(0, 64)],
            dst_ref=hext.at[pl.ds(192, 64)],
            send_sem=h_send.at[1],
            recv_sem=h_recv.at[1],
            device_id={"patch": me_p - 1, "ens": me},
            device_id_type=MESH,
        )

    def cut(ref, index, first):
        row = lax.rem(index, row_cuts) * piece_rows + first
        column = pl.multiple_of((index // row_cuts) * piece_cols, 128)
        return ref.at[pl.ds(pl.multiple_of(row, 16), piece_rows), pl.ds(column, piece_cols)]

    def to_relay(index, first, side):
        return pltpu.make_async_remote_copy(
            src_ref=cut(h1, index, first),
            dst_ref=relay,
            send_sem=x_send.at[index],
            recv_sem=relay_recv,
            device_id={"patch": relay_patch(side, index, half), "ens": me},
            device_id_type=MESH,
        )

    def each_halo(act):
        @pl.when(has_right)
        def _():
            act(send_tail())

        @pl.when(has_left)
        def _():
            act(send_head())

        @pl.when(me_p == half - 1)
        def _():
            lax.fori_loop(0, relays, lambda i, c: (act(to_relay(i, 64, tail_side)), c)[1], 0)

        @pl.when(me_p == half)
        def _():
            lax.fori_loop(0, relays, lambda i, c: (act(to_relay(i, 0, head_side)), c)[1], 0)

    each_halo(lambda copy: copy.start())

    def onward(index, first, patch, slot):
        return pltpu.make_async_remote_copy(
            src_ref=relay,
            dst_ref=cut(hext, index, first),
            send_sem=relay_send,
            recv_sem=h_recv.at[slot],
            device_id={"patch": patch, "ens": me},
            device_id_type=MESH,
        )

    def forward_tail():
        return onward(jnp.where(tail_relay, tail_index, 0), 0, half, 0)

    def forward_head():
        return onward(jnp.where(head_relay, head_index, 0), 192, half - 1, 1)

    for first in range(0, 256, 128):
        rows = slice(first, first + 128)
        slots = lax.broadcasted_iota(jnp.int32, (128, 256), 0) + first
        cos_map = jnp.zeros((128, 256), jnp.float32)
        sin_map = jnp.zeros((128, 256), jnp.float32)
        for column in range(K):
            cosine, sine = turn_table(turns[column])
            hit = links[column] == slots
            cos_map += jnp.where(hit, cosine, 0.0)
            sin_map += jnp.where(hit, sine, 0.0)
        tmaps[0, rows] = cos_map.astype(jnp.bfloat16)
        tmaps[1, rows] = sin_map.astype(jnp.bfloat16)
        maps[0, :, rows] = cos_map.T.astype(jnp.bfloat16)
        maps[1, :, rows] = sin_map.T.astype(jnp.bfloat16)

    @pl.when(me_p == 0)
    def _():
        hext[0:64] = jnp.zeros((64, hext.shape[1]), hext.dtype)

    @pl.when(me_p == last)
    def _():
        hext[192:256] = jnp.zeros((64, hext.shape[1]), hext.dtype)

    @pl.when(head_relay)
    def _():
        pltpu.make_async_copy(relay, relay, relay_recv).wait()
        forward_head().start()

    outside = (low & (me_p == 0)) | (high & (me_p == last))

    def side_of(left, right):
        return jnp.where(left > right, 1.0, jnp.where(left < right, -1.0, 0.0))

    def send_grad(i):
        to = lax.rem(me + i, members)
        return pltpu.make_async_remote_copy(
            src_ref=gout.at[to],
            dst_ref=gext.at[jnp.where(scorer, place, 0)],
            send_sem=g_send.at[i],
            recv_sem=g_sem,
            device_id={"patch": me_p, "ens": to},
            device_id_type=MESH,
        )

    def send_across(i, patch, share_index):
        to = lax.rem(me + i, members)
        return pltpu.make_async_remote_copy(
            src_ref=gout.at[to],
            dst_ref=gext.at[share_index],
            send_sem=c_send.at[i],
            recv_sem=g_sem,
            device_id={"patch": patch, "ens": to},
            device_id_type=MESH,
        )

    def send_up(i):
        return send_across(i, half, jnp.where(tail_scorer, place - pieces, 0))

    def send_down(i):
        return send_across(i, half - 1, jnp.where(head_scorer, place + pieces, 0))

    idle = (low & over) | (high & under)

    @pl.when(scorer & idle)
    def _():
        pl.semaphore_wait(ready, members - 1)

    @pl.when(scorer & jnp.logical_not(idle))
    def _():
        @pl.when(outside)
        def _():
            pin[...] = jnp.zeros(pin.shape, pin.dtype)
            tin[...] = jnp.zeros(tin.shape, tin.dtype)

        @pl.when(jnp.logical_not(outside))
        def _():
            with jax.named_scope("wait_pred"):
                pltpu.make_async_copy(pin, pin, pin_sem).wait()
                pltpu.make_async_copy(tin, tin, tin_sem).wait()

        with jax.named_scope("score"):
            for first in range(0, share, 16):
                rows = slice(first, first + 16)
                values = pin[:, rows].astype(jnp.float32)
                observed = tin[rows].astype(jnp.float32)
                total = jnp.zeros(values.shape, jnp.float32)
                for shift in range(1, members // 2 + 1):
                    other = jnp.concatenate([values[shift:], values[:shift]], axis=0)
                    side = side_of(values, other)
                    total += side
                    if shift < members // 2:
                        total -= jnp.concatenate(
                            [side[members - shift :], side[: members - shift]], axis=0
                        )
                own_side = side_of(values, observed[None])
                gout[:, rows] = (own_side - total / (members - 1)).astype(jnp.bfloat16)
        with jax.named_scope("send_grad"):

            @pl.when(head_scorer)
            def _():
                lax.fori_loop(0, members, lambda i, c: (send_down(i).start(), c)[1], 0)

            pl.semaphore_wait(ready, members - 1)
            lax.fori_loop(1, members, lambda i, c: (send_grad(i).start(), c)[1], 0)
            pltpu.make_async_copy(
                gout.at[me], gext.at[jnp.where(scorer, place, 0)], g_sem
            ).start()

    load_w2.wait()
    w2c[0:512, 0:128] = w2v[0:512]
    w2c[0:512, 128:256] = w2v[512:1024]
    w2c[512:1024, 0:128] = w2v[512:1024]
    w2c[512:1024, 128:256] = -w2v[0:512]

    own_h.wait()

    @pl.when(me_p > 0)
    def _():
        pltpu.make_async_copy(hext.at[pl.ds(0, 64)], hext.at[pl.ds(0, 64)], h_recv.at[0]).wait()

    @pl.when(tail_scorer)
    def _():
        pl.semaphore_wait(cross, members)
        lax.fori_loop(0, members, lambda i, c: (send_up(i).start(), c)[1], 0)

    @pl.when(me_p < last)
    def _():
        pltpu.make_async_copy(
            hext.at[pl.ds(192, 64)], hext.at[pl.ds(192, 64)], h_recv.at[1]
        ).wait()

    features = hext[...]
    by_cos = jnp.dot(maps[0, 32:224], features, preferred_element_type=jnp.float32)
    by_sin = jnp.dot(maps[1, 32:224], features, preferred_element_type=jnp.float32)
    summed = jnp.concatenate(
        [
            (by_cos[:, :512] - by_sin[:, 512:]).astype(jnp.bfloat16),
            (by_sin[:, :512] + by_cos[:, 512:]).astype(jnp.bfloat16),
        ],
        axis=1,
    )
    load_w1.wait()
    pre_act = jnp.dot(summed, w1v[...], preferred_element_type=jnp.float32)
    sigmoid = jax.nn.sigmoid(pre_act)
    deriv[...] = sigmoid * (1.0 + pre_act * (1.0 - sigmoid))
    back[0:32] = jnp.zeros((32, back.shape[1]), back.dtype)
    back[224:256] = jnp.zeros((32, back.shape[1]), back.dtype)

    pltpu.make_async_copy(gext, gext, g_sem).wait()
    grads = gext[...].reshape(256, 128)
    spread_grads = jnp.concatenate(
        [
            jnp.dot(tmaps[0, 32:224], grads, preferred_element_type=jnp.float32),
            jnp.dot(tmaps[1, 32:224], grads, preferred_element_type=jnp.float32),
        ],
        axis=1,
    ).astype(jnp.bfloat16)
    contract_last = (((1,), (1,)), ((), ()))
    gmid[...] = lax.dot_general(
        spread_grads, w2c[...], contract_last, preferred_element_type=jnp.float32
    )
    act_grad = (gmid[...] * deriv[...]).astype(jnp.bfloat16)
    back[32:224] = lax.dot_general(
        act_grad, w1v[...], contract_last, preferred_element_type=jnp.float32
    ).astype(jnp.bfloat16)
    rows_back = back[...]
    by_cos = jnp.dot(tmaps[0, 64:192], rows_back, preferred_element_type=jnp.float32)
    by_sin = jnp.dot(tmaps[1, 64:192], rows_back, preferred_element_type=jnp.float32)
    out[:, :512] = (gmid[32:160, :512] + by_cos[:, :512] + by_sin[:, 512:]).astype(out.dtype)
    out[:, 512:] = (gmid[32:160, 512:] + by_cos[:, 512:] - by_sin[:, :512]).astype(out.dtype)

    @pl.when(tail_relay)
    def _():
        pltpu.make_async_copy(relay, relay, relay_recv).wait()
        pl.semaphore_wait(cross, 1)
        forward_tail().start()

    @pl.when(tail_relay)
    def _():
        forward_tail().wait_send()

    @pl.when(head_relay)
    def _():
        forward_head().wait_send()

    @pl.when(tail_scorer)
    def _():
        lax.fori_loop(0, members, lambda i, c: (send_up(i).wait_send(), c)[1], 0)

    @pl.when(head_scorer)
    def _():
        lax.fori_loop(0, members, lambda i, c: (send_down(i).wait_send(), c)[1], 0)

    each_pred(lambda copy: copy.wait_send())
    each_target(lambda copy: copy.wait_send())
    each_halo(lambda copy: copy.wait_send())

    @pl.when(scorer & jnp.logical_not(idle))
    def _():
        lax.fori_loop(1, members, lambda i, c: (send_grad(i).wait_send(), c)[1], 0)


def per_device(pred, target, h1, w1, w2, neighbours, rotations):
    members = lax.axis_size("ens")
    patches = lax.axis_size("patch")
    rows, channels = h1.shape[1:]
    scorers = members // 2
    share = 256 // scorers
    relays = 4 if patches >= 64 else 1
    row_cuts = min(4, relays)
    anywhere = pl.BlockSpec(memory_space=pltpu.HBM)
    vmem = pl.BlockSpec(memory_space=pltpu.VMEM)
    dma = pltpu.SemaphoreType.DMA
    bf16 = jnp.bfloat16
    result = pl.pallas_call(
        functools.partial(kernel, patches, members),
        out_shape=jax.ShapeDtypeStruct((rows, channels), bf16),
        in_specs=[anywhere, anywhere, anywhere, anywhere, anywhere, vmem, vmem],
        out_specs=vmem,
        scratch_shapes=[
            pltpu.VMEM((256, channels), bf16),
            pltpu.VMEM((members, share, 128), bf16),
            pltpu.VMEM((share, 128), bf16),
            pltpu.VMEM((members, share, 128), bf16),
            pltpu.VMEM((scorers, share, 128), bf16),
            pltpu.VMEM((channels, channels), bf16),
            pltpu.VMEM((channels, 128), bf16),
            pltpu.VMEM((channels, 256), bf16),
            pltpu.VMEM((2, 256, 256), bf16),
            pltpu.VMEM((2, 256, 256), bf16),
            pltpu.VMEM((192, channels), jnp.float32),
            pltpu.VMEM((192, channels), jnp.float32),
            pltpu.VMEM((256, channels), bf16),
            pltpu.VMEM((64 // row_cuts, channels * row_cuts // relays), bf16),
            dma((3,)),
            dma(()),
            dma(()),
            dma((members,)),
            dma(()),
            dma(()),
            dma((members,)),
            dma((2,)),
            dma((2,)),
            dma((relays,)),
            dma(()),
            dma(()),
            pltpu.SemaphoreType.REGULAR,
            pltpu.SemaphoreType.REGULAR,
            dma((members,)),
        ],
        compiler_params=pltpu.CompilerParams(
            collective_id=0, has_side_effects=True, vmem_limit_bytes=62 * 2**20
        ),
        name="mesh_backward",
    )(
        pred[0],
        target,
        h1[0],
        w1,
        w2,
        jnp.transpose(neighbours, (2, 0, 1)),
        jnp.transpose(rotations, (2, 0, 1)),
    )
    return result[None]


def solution(mesh):
    return jax.shard_map(
        per_device,
        mesh=mesh,
        in_specs=(
            P("ens", "patch", None),
            P("patch", None),
            P("ens", "patch", None),
            P(),
            P(),
            P("patch", None, None),
            P("patch", None, None),
        ),
        out_specs=P("ens", "patch", None),
        check_vma=False,
    )
```

```python
import functools

import jax
import jax.numpy as jnp
from jax import lax
from jax.experimental import pallas as pl
from jax.experimental.pallas import tpu as pltpu
from jax.sharding import PartitionSpec as P

K = 6
H = 32
MESH = pl.DeviceIdType.MESH


def relay_patches(side, half):
    if half < 32:
        return (half - 1 + half,) if side else (0,)
    return (40, 63, 56, 39) if side else (23, 24, 7, 0)


def relay_patch(side, index, half):
    patches = relay_patches(side, half)
    patch = jnp.int32(patches[0])
    for i, other in enumerate(patches):
        patch = jnp.where(index == i, other, patch)
    return patch


def relay_job(side, patch, half):
    mine, index = patch < 0, jnp.int32(0)
    for i, other in enumerate(relay_patches(side, half)):
        mine = mine | (patch == other)
        index = jnp.where(patch == other, i, index)
    return mine, index


def turn_table(turns):
    diag = jnp.float32(0.70710678118654752)
    zero = jnp.zeros(turns.shape, jnp.float32)
    one = zero + 1.0

    def cosine(r):
        return jnp.where(
            r == 0,
            one,
            jnp.where(
                (r == 1) | (r == 7),
                zero + diag,
                jnp.where((r == 2) | (r == 6), zero, jnp.where(r == 4, -one, zero - diag)),
            ),
        )

    return cosine(turns), cosine((turns + 6) & 7)


def kernel(
    patches,
    members,
    pred,
    target,
    h1,
    w1,
    w2,
    links,
    turns,
    out,
    hext,
    pin,
    tin,
    gout,
    gext,
    w1v,
    w2v,
    w2c,
    maps,
    tmaps,
    deriv,
    gmid,
    back,
    relay,
    load_sem,
    pin_sem,
    tin_sem,
    pred_send,
    tgt_send,
    g_sem,
    g_send,
    h_recv,
    h_send,
    x_send,
    relay_recv,
    relay_send,
    ready,
    cross,
    c_send,
):
    me_p = lax.axis_index("patch")
    me = lax.axis_index("ens")
    half = patches // 2
    scorers = members // 2
    share = 256 // scorers
    pieces = scorers // 2
    quarter = scorers // 4
    base = members // 4
    relays = x_send.shape[0]
    row_cuts = min(4, relays)
    piece_rows, piece_cols = relay.shape
    last = patches - 1
    place = me - base
    scorer = (place >= 0) & (place < scorers)
    low = scorer & (place < quarter)
    high = scorer & (place >= scorers - quarter)
    middle = (place >= quarter) & (place < scorers - quarter)
    tail_side, head_side = 0, 1
    under, over = me_p == half - 1, me_p == half
    has_left = (me_p > 0) & jnp.logical_not(over)
    has_right = (me_p < last) & jnp.logical_not(under)
    tail_scorer = under & middle & (place >= pieces)
    head_scorer = over & middle & (place < pieces)
    tail_relay, tail_index = relay_job(tail_side, me_p, half)
    head_relay, head_index = relay_job(head_side, me_p, half)

    own_h = pltpu.make_async_copy(h1, hext.at[pl.ds(64, 128)], load_sem.at[0])
    own_h.start()
    load_w2 = pltpu.make_async_copy(w2, w2v, load_sem.at[1])
    load_w2.start()
    load_w1 = pltpu.make_async_copy(w1, w1v, load_sem.at[2])
    load_w1.start()

    barrier = pltpu.get_barrier_semaphore()

    def greet(patch, ens):
        pl.semaphore_signal(
            barrier, inc=1, device_id={"patch": patch, "ens": ens}, device_id_type=MESH
        )

    def greet_own(i, carry):
        greet(me_p, lax.rem(me + i, members))
        return carry

    @pl.when(scorer)
    def _():
        lax.fori_loop(1, members, greet_own, 0)

    @pl.when(low & has_left)
    def _():
        lax.fori_loop(0, members, lambda i, c: (greet(me_p - 1, i), c)[1], 0)

    @pl.when(high & has_right)
    def _():
        lax.fori_loop(0, members, lambda i, c: (greet(me_p + 1, i), c)[1], 0)

    @pl.when(has_left)
    def _():
        greet(me_p - 1, me)

    @pl.when(has_right)
    def _():
        greet(me_p + 1, me)

    @pl.when(under)
    def _():
        lax.fori_loop(
            0, relays, lambda i, c: (greet(relay_patch(head_side, i, half), me), c)[1], 0
        )
        lax.fori_loop(quarter, pieces, lambda i, c: (greet(half, base + i), c)[1], 0)

    @pl.when(tail_scorer)
    def _():
        lax.fori_loop(0, members, lambda i, c: (greet(half + 1, i), c)[1], 0)

    @pl.when(tail_relay)
    def _():
        greet(half - 1, me)
        greet(half + 1, me)

    @pl.when(head_relay)
    def _():
        greet(half, me)

    def count(flag, amount):
        return jnp.where(flag, amount, 0)

    partners = (
        scorers
        - count(scorer, 1)
        + count(has_right, quarter)
        + count(has_left, quarter)
        + count(me_p < last, count(me_p == half - 1, relays - 1) + 1)
        + count(me_p > 0, count(me_p == half, relays - 1) + 1)
        + count(me_p == half + 1, relays + quarter)
        + count(head_scorer, members)
        + count(head_relay, 1)
    )
    pl.semaphore_wait(barrier, partners)

    def send_pred(piece, patch, to, slot):
        return pltpu.make_async_remote_copy(
            src_ref=pred.at[pl.ds(pl.multiple_of(piece * share, 16), share)],
            dst_ref=pin.at[me],
            send_sem=pred_send.at[slot],
            recv_sem=pin_sem,
            device_id={"patch": patch, "ens": base + to},
            device_id_type=MESH,
        )

    def each_pred(act):
        def across(i, carry):
            piece = lax.rem(me + i, pieces)
            upper = piece >= quarter

            @pl.when(upper & has_right)
            def _():
                act(send_pred(piece, me_p + 1, piece - quarter, pieces + piece))

            @pl.when(jnp.logical_not(upper) & has_left)
            def _():
                act(send_pred(piece, me_p - 1, scorers - quarter + piece, pieces + piece))

            @pl.when(piece + quarter != place)
            def _():
                act(send_pred(piece, me_p, piece + quarter, piece))

            return carry

        lax.fori_loop(0, pieces, across, 0)

    each_pred(lambda copy: copy.start())

    def tell(i, carry):
        @pl.when(i != place)
        def _():
            pl.semaphore_signal(
                ready, inc=1, device_id={"patch": me_p, "ens": base + i}, device_id_type=MESH
            )

        return carry

    lax.fori_loop(0, scorers, tell, 0)

    def tell_across(patch, ens):
        pl.semaphore_signal(
            cross, inc=1, device_id={"patch": patch, "ens": ens}, device_id_type=MESH
        )

    @pl.when(me_p == half + 1)
    def _():
        lax.fori_loop(
            0, relays, lambda i, c: (tell_across(relay_patch(tail_side, i, half), me), c)[1], 0
        )
        lax.fori_loop(
            pieces, pieces + quarter, lambda i, c: (tell_across(half - 1, base + i), c)[1], 0
        )

    def send_target(first, patch):
        return pltpu.make_async_remote_copy(
            src_ref=target.at[pl.ds(pl.multiple_of(first, 16), share)],
            dst_ref=tin,
            send_sem=tgt_send,
            recv_sem=tin_sem,
            device_id={"patch": patch, "ens": me},
            device_id_type=MESH,
        )

    def each_target(act):
        @pl.when(low & has_right)
        def _():
            act(send_target((quarter + jnp.where(low, place, 0)) * share, me_p + 1))

        @pl.when(high & has_left)
        def _():
            act(send_target(jnp.where(high, place - (scorers - quarter), 0) * share, me_p - 1))

    each_target(lambda copy: copy.start())

    @pl.when(middle)
    def _():
        own = pl.ds(pl.multiple_of(jnp.where(middle, place - quarter, 0) * share, 16), share)
        pltpu.make_async_copy(pred.at[own], pin.at[me], pin_sem).start()
        pltpu.make_async_copy(target.at[own], tin, tin_sem).start()

    def send_tail():
        return pltpu.make_async_remote_copy(
            src_ref=h1.at[pl.ds(64, 64)],
            dst_ref=hext.at[pl.ds(0, 64)],
            send_sem=h_send.at[0],
            recv_sem=h_recv.at[0],
            device_id={"patch": me_p + 1, "ens": me},
            device_id_type=MESH,
        )

    def send_head():
        return pltpu.make_async_remote_copy(
            src_ref=h1.at[pl.ds(0, 64)],
            dst_ref=hext.at[pl.ds(192, 64)],
            send_sem=h_send.at[1],
            recv_sem=h_recv.at[1],
            device_id={"patch": me_p - 1, "ens": me},
            device_id_type=MESH,
        )

    def cut(ref, index, first):
        row = lax.rem(index, row_cuts) * piece_rows + first
        column = pl.multiple_of((index // row_cuts) * piece_cols, 128)
        return ref.at[pl.ds(pl.multiple_of(row, 16), piece_rows), pl.ds(column, piece_cols)]

    def to_relay(index, first, side):
        return pltpu.make_async_remote_copy(
            src_ref=cut(h1, index, first),
            dst_ref=relay,
            send_sem=x_send.at[index],
            recv_sem=relay_recv,
            device_id={"patch": relay_patch(side, index, half), "ens": me},
            device_id_type=MESH,
        )

    def each_halo(act):
        @pl.when(has_right)
        def _():
            act(send_tail())

        @pl.when(has_left)
        def _():
            act(send_head())

        @pl.when(me_p == half - 1)
        def _():
            lax.fori_loop(0, relays, lambda i, c: (act(to_relay(i, 64, tail_side)), c)[1], 0)

        @pl.when(me_p == half)
        def _():
            lax.fori_loop(0, relays, lambda i, c: (act(to_relay(i, 0, head_side)), c)[1], 0)

    each_halo(lambda copy: copy.start())

    def onward(index, first, patch, slot):
        return pltpu.make_async_remote_copy(
            src_ref=relay,
            dst_ref=cut(hext, index, first),
            send_sem=relay_send,
            recv_sem=h_recv.at[slot],
            device_id={"patch": patch, "ens": me},
            device_id_type=MESH,
        )

    def forward_tail():
        return onward(jnp.where(tail_relay, tail_index, 0), 0, half, 0)

    def forward_head():
        return onward(jnp.where(head_relay, head_index, 0), 192, half - 1, 1)

    for first in range(0, 256, 128):
        rows = slice(first, first + 128)
        slots = lax.broadcasted_iota(jnp.int32, (128, 256), 0) + first
        cos_map = jnp.zeros((128, 256), jnp.float32)
        sin_map = jnp.zeros((128, 256), jnp.float32)
        for column in range(K):
            cosine, sine = turn_table(turns[column])
            hit = links[column] == slots
            cos_map += jnp.where(hit, cosine, 0.0)
            sin_map += jnp.where(hit, sine, 0.0)
        tmaps[0, rows] = cos_map.astype(jnp.bfloat16)
        tmaps[1, rows] = sin_map.astype(jnp.bfloat16)
        maps[0, :, rows] = cos_map.T.astype(jnp.bfloat16)
        maps[1, :, rows] = sin_map.T.astype(jnp.bfloat16)

    @pl.when(me_p == 0)
    def _():
        hext[0:64] = jnp.zeros((64, hext.shape[1]), hext.dtype)

    @pl.when(me_p == last)
    def _():
        hext[192:256] = jnp.zeros((64, hext.shape[1]), hext.dtype)

    @pl.when(head_relay)
    def _():
        pltpu.make_async_copy(relay, relay, relay_recv).wait()
        forward_head().start()

    outside = (low & (me_p == 0)) | (high & (me_p == last))

    def side_of(left, right):
        return jnp.where(left > right, 1.0, jnp.where(left < right, -1.0, 0.0))

    def send_grad(to):
        return pltpu.make_async_remote_copy(
            src_ref=gout.at[to],
            dst_ref=gext.at[jnp.where(scorer, place, 0)],
            send_sem=g_send.at[to],
            recv_sem=g_sem,
            device_id={"patch": me_p, "ens": to},
            device_id_type=MESH,
        )

    def each_grad(act):
        def one(to, carry):
            @pl.when(to != me)
            def _():
                act(send_grad(to))

            return carry

        lax.fori_loop(0, members, one, 0)

    def send_across(to, patch, share_index):
        return pltpu.make_async_remote_copy(
            src_ref=gout.at[to],
            dst_ref=gext.at[share_index],
            send_sem=c_send.at[to],
            recv_sem=g_sem,
            device_id={"patch": patch, "ens": to},
            device_id_type=MESH,
        )

    def send_up(i):
        return send_across(i, half, jnp.where(tail_scorer, place - pieces, 0))

    def send_down(i):
        return send_across(i, half - 1, jnp.where(head_scorer, place + pieces, 0))

    idle = (low & over) | (high & under)

    @pl.when(scorer & idle)
    def _():
        pl.semaphore_wait(ready, members - 1)

    @pl.when(scorer & jnp.logical_not(idle))
    def _():
        @pl.when(outside)
        def _():
            pin[...] = jnp.zeros(pin.shape, pin.dtype)
            tin[...] = jnp.zeros(tin.shape, tin.dtype)

        @pl.when(jnp.logical_not(outside))
        def _():
            with jax.named_scope("wait_pred"):
                pltpu.make_async_copy(pin, pin, pin_sem).wait()
                pltpu.make_async_copy(tin, tin, tin_sem).wait()

        with jax.named_scope("score"):
            for first in range(0, share, 16):
                rows = slice(first, first + 16)
                values = pin[:, rows].astype(jnp.float32)
                observed = tin[rows].astype(jnp.float32)
                total = jnp.zeros(values.shape, jnp.float32)
                for shift in range(1, members // 2 + 1):
                    other = jnp.concatenate([values[shift:], values[:shift]], axis=0)
                    side = side_of(values, other)
                    total += side
                    if shift < members // 2:
                        total -= jnp.concatenate(
                            [side[members - shift :], side[: members - shift]], axis=0
                        )
                own_side = side_of(values, observed[None])
                gout[:, rows] = (own_side - total / (members - 1)).astype(jnp.bfloat16)
        with jax.named_scope("send_grad"):

            @pl.when(head_scorer)
            def _():
                lax.fori_loop(0, members, lambda i, c: (send_down(i).start(), c)[1], 0)

            pl.semaphore_wait(ready, members - 1)
            each_grad(lambda copy: copy.start())
            pltpu.make_async_copy(
                gout.at[me], gext.at[jnp.where(scorer, place, 0)], g_sem
            ).start()

    load_w2.wait()
    w2c[0:512, 0:128] = w2v[0:512]
    w2c[0:512, 128:256] = w2v[512:1024]
    w2c[512:1024, 0:128] = w2v[512:1024]
    w2c[512:1024, 128:256] = -w2v[0:512]

    own_h.wait()

    @pl.when(me_p > 0)
    def _():
        pltpu.make_async_copy(hext.at[pl.ds(0, 64)], hext.at[pl.ds(0, 64)], h_recv.at[0]).wait()

    @pl.when(tail_scorer)
    def _():
        pl.semaphore_wait(cross, members)
        lax.fori_loop(0, members, lambda i, c: (send_up(i).start(), c)[1], 0)

    @pl.when(me_p < last)
    def _():
        pltpu.make_async_copy(
            hext.at[pl.ds(192, 64)], hext.at[pl.ds(192, 64)], h_recv.at[1]
        ).wait()

    features = hext[...]
    by_cos = jnp.dot(maps[0, 32:224], features, preferred_element_type=jnp.float32)
    by_sin = jnp.dot(maps[1, 32:224], features, preferred_element_type=jnp.float32)
    summed = jnp.concatenate(
        [
            (by_cos[:, :512] - by_sin[:, 512:]).astype(jnp.bfloat16),
            (by_sin[:, :512] + by_cos[:, 512:]).astype(jnp.bfloat16),
        ],
        axis=1,
    )
    load_w1.wait()
    pre_act = jnp.dot(summed, w1v[...], preferred_element_type=jnp.float32)
    sigmoid = jax.nn.sigmoid(pre_act)
    deriv[...] = sigmoid * (1.0 + pre_act * (1.0 - sigmoid))
    back[0:32] = jnp.zeros((32, back.shape[1]), back.dtype)
    back[224:256] = jnp.zeros((32, back.shape[1]), back.dtype)

    pltpu.make_async_copy(gext, gext, g_sem).wait()
    grads = gext[...].reshape(256, 128)
    spread_grads = jnp.concatenate(
        [
            jnp.dot(tmaps[0, 32:224], grads, preferred_element_type=jnp.float32),
            jnp.dot(tmaps[1, 32:224], grads, preferred_element_type=jnp.float32),
        ],
        axis=1,
    ).astype(jnp.bfloat16)
    contract_last = (((1,), (1,)), ((), ()))
    gmid[...] = lax.dot_general(
        spread_grads, w2c[...], contract_last, preferred_element_type=jnp.float32
    )
    act_grad = (gmid[...] * deriv[...]).astype(jnp.bfloat16)
    back[32:224] = lax.dot_general(
        act_grad, w1v[...], contract_last, preferred_element_type=jnp.float32
    ).astype(jnp.bfloat16)
    rows_back = back[...]
    by_cos = jnp.dot(tmaps[0, 64:192], rows_back, preferred_element_type=jnp.float32)
    by_sin = jnp.dot(tmaps[1, 64:192], rows_back, preferred_element_type=jnp.float32)
    out[:, :512] = (gmid[32:160, :512] + by_cos[:, :512] + by_sin[:, 512:]).astype(out.dtype)
    out[:, 512:] = (gmid[32:160, 512:] + by_cos[:, 512:] - by_sin[:, :512]).astype(out.dtype)

    @pl.when(tail_relay)
    def _():
        pltpu.make_async_copy(relay, relay, relay_recv).wait()
        pl.semaphore_wait(cross, 1)
        forward_tail().start()

    @pl.when(tail_relay)
    def _():
        forward_tail().wait_send()

    @pl.when(head_relay)
    def _():
        forward_head().wait_send()

    @pl.when(tail_scorer)
    def _():
        lax.fori_loop(0, members, lambda i, c: (send_up(i).wait_send(), c)[1], 0)

    @pl.when(head_scorer)
    def _():
        lax.fori_loop(0, members, lambda i, c: (send_down(i).wait_send(), c)[1], 0)

    each_pred(lambda copy: copy.wait_send())
    each_target(lambda copy: copy.wait_send())
    each_halo(lambda copy: copy.wait_send())

    @pl.when(scorer & jnp.logical_not(idle))
    def _():
        each_grad(lambda copy: copy.wait_send())


def per_device(pred, target, h1, w1, w2, neighbours, rotations):
    members = lax.axis_size("ens")
    patches = lax.axis_size("patch")
    rows, channels = h1.shape[1:]
    scorers = members // 2
    share = 256 // scorers
    relays = 4 if patches >= 64 else 1
    row_cuts = min(4, relays)
    anywhere = pl.BlockSpec(memory_space=pltpu.HBM)
    vmem = pl.BlockSpec(memory_space=pltpu.VMEM)
    dma = pltpu.SemaphoreType.DMA
    bf16 = jnp.bfloat16
    result = pl.pallas_call(
        functools.partial(kernel, patches, members),
        out_shape=pltpu.VMEM((rows, channels), bf16),
        in_specs=[anywhere, anywhere, anywhere, anywhere, anywhere, vmem, vmem],
        out_specs=vmem,
        scratch_shapes=[
            pltpu.VMEM((256, channels), bf16),
            pltpu.VMEM((members, share, 128), bf16),
            pltpu.VMEM((share, 128), bf16),
            pltpu.VMEM((members, share, 128), bf16),
            pltpu.VMEM((scorers, share, 128), bf16),
            pltpu.VMEM((channels, channels), bf16),
            pltpu.VMEM((channels, 128), bf16),
            pltpu.VMEM((channels, 256), bf16),
            pltpu.VMEM((2, 256, 256), bf16),
            pltpu.VMEM((2, 256, 256), bf16),
            pltpu.VMEM((192, channels), jnp.float32),
            pltpu.VMEM((192, channels), jnp.float32),
            pltpu.VMEM((256, channels), bf16),
            pltpu.VMEM((64 // row_cuts, channels * row_cuts // relays), bf16),
            dma((3,)),
            dma(()),
            dma(()),
            dma((members,)),
            dma(()),
            dma(()),
            dma((members,)),
            dma((2,)),
            dma((2,)),
            dma((relays,)),
            dma(()),
            dma(()),
            pltpu.SemaphoreType.REGULAR,
            pltpu.SemaphoreType.REGULAR,
            dma((members,)),
        ],
        compiler_params=pltpu.CompilerParams(
            collective_id=0, has_side_effects=True, vmem_limit_bytes=62 * 2**20
        ),
        name="mesh_backward",
    )(
        pred[0],
        target,
        h1[0],
        w1,
        w2,
        jnp.transpose(neighbours, (2, 0, 1)),
        jnp.transpose(rotations, (2, 0, 1)),
    )
    return result[None]


def solution(mesh):
    return jax.shard_map(
        per_device,
        mesh=mesh,
        in_specs=(
            P("ens", "patch", None),
            P("patch", None),
            P("ens", "patch", None),
            P(),
            P(),
            P("patch", None, None),
            P("patch", None, None),
        ),
        out_specs=P("ens", "patch", None),
        check_vma=False,
    )
```

```python
import functools

import jax
import jax.numpy as jnp
from jax import lax
from jax.experimental import pallas as pl
from jax.experimental.pallas import tpu as pltpu
from jax.sharding import PartitionSpec as P

K = 6
H = 32
MESH = pl.DeviceIdType.MESH


def relay_patches(side, half):
    if half < 32:
        return (half - 1 + half,) if side else (0,)
    return (40, 63, 56, 39) if side else (23, 24, 7, 0)


def relay_patch(side, index, half):
    patches = relay_patches(side, half)
    patch = jnp.int32(patches[0])
    for i, other in enumerate(patches):
        patch = jnp.where(index == i, other, patch)
    return patch


def relay_job(side, patch, half):
    mine, index = patch < 0, jnp.int32(0)
    for i, other in enumerate(relay_patches(side, half)):
        mine = mine | (patch == other)
        index = jnp.where(patch == other, i, index)
    return mine, index


def turn_table(turns):
    diag = jnp.float32(0.70710678118654752)
    zero = jnp.zeros(turns.shape, jnp.float32)
    one = zero + 1.0

    def cosine(r):
        return jnp.where(
            r == 0,
            one,
            jnp.where(
                (r == 1) | (r == 7),
                zero + diag,
                jnp.where((r == 2) | (r == 6), zero, jnp.where(r == 4, -one, zero - diag)),
            ),
        )

    return cosine(turns), cosine((turns + 6) & 7)


def kernel(
    patches,
    members,
    pred,
    target,
    h1,
    w1,
    w2,
    links_in,
    turns_in,
    out,
    hext,
    pin,
    tin,
    gout,
    gext,
    w1v,
    w2v,
    w2c,
    maps,
    tmaps,
    deriv,
    gmid,
    back,
    relay,
    load_sem,
    pin_sem,
    tin_sem,
    pred_send,
    tgt_send,
    g_sem,
    g_send,
    h_recv,
    h_send,
    x_send,
    relay_recv,
    relay_send,
    ready,
    cross,
    c_send,
    links,
    turns,
):
    me_p = lax.axis_index("patch")
    me = lax.axis_index("ens")
    half = patches // 2
    scorers = members // 2
    share = 256 // scorers
    pieces = scorers // 2
    quarter = scorers // 4
    base = members // 4
    relays = x_send.shape[0]
    row_cuts = min(4, relays)
    piece_rows, piece_cols = relay.shape
    last = patches - 1
    place = me - base
    scorer = (place >= 0) & (place < scorers)
    low = scorer & (place < quarter)
    high = scorer & (place >= scorers - quarter)
    middle = (place >= quarter) & (place < scorers - quarter)
    tail_side, head_side = 0, 1
    under, over = me_p == half - 1, me_p == half
    has_left = (me_p > 0) & jnp.logical_not(over)
    has_right = (me_p < last) & jnp.logical_not(under)
    tail_scorer = under & middle & (place >= pieces)
    head_scorer = over & middle & (place < pieces)
    tail_relay, tail_index = relay_job(tail_side, me_p, half)
    head_relay, head_index = relay_job(head_side, me_p, half)

    barrier = pltpu.get_barrier_semaphore()

    def greet(patch, ens):
        pl.semaphore_signal(
            barrier, inc=1, device_id={"patch": patch, "ens": ens}, device_id_type=MESH
        )

    def greet_own(i, carry):
        greet(me_p, lax.rem(me + i, members))
        return carry

    @pl.when(scorer)
    def _():
        lax.fori_loop(1, members, greet_own, 0)

    @pl.when(low & has_left)
    def _():
        lax.fori_loop(0, members, lambda i, c: (greet(me_p - 1, i), c)[1], 0)

    @pl.when(high & has_right)
    def _():
        lax.fori_loop(0, members, lambda i, c: (greet(me_p + 1, i), c)[1], 0)

    @pl.when(has_left)
    def _():
        greet(me_p - 1, me)

    @pl.when(has_right)
    def _():
        greet(me_p + 1, me)

    @pl.when(under)
    def _():
        lax.fori_loop(
            0, relays, lambda i, c: (greet(relay_patch(head_side, i, half), me), c)[1], 0
        )
        lax.fori_loop(quarter, pieces, lambda i, c: (greet(half, base + i), c)[1], 0)

    @pl.when(tail_scorer)
    def _():
        lax.fori_loop(0, members, lambda i, c: (greet(half + 1, i), c)[1], 0)

    @pl.when(tail_relay)
    def _():
        greet(half - 1, me)
        greet(half + 1, me)

    @pl.when(head_relay)
    def _():
        greet(half, me)

    def count(flag, amount):
        return jnp.where(flag, amount, 0)

    partners = (
        scorers
        - count(scorer, 1)
        + count(has_right, quarter)
        + count(has_left, quarter)
        + count(me_p < last, count(me_p == half - 1, relays - 1) + 1)
        + count(me_p > 0, count(me_p == half, relays - 1) + 1)
        + count(me_p == half + 1, relays + quarter)
        + count(head_scorer, members)
        + count(head_relay, 1)
    )
    own_h = pltpu.make_async_copy(h1, hext.at[pl.ds(64, 128)], load_sem.at[0])
    own_h.start()
    load_w2 = pltpu.make_async_copy(w2, w2v, load_sem.at[1])
    load_w2.start()
    load_w1 = pltpu.make_async_copy(w1, w1v, load_sem.at[2])
    load_w1.start()
    load_links = pltpu.make_async_copy(links_in, links, load_sem.at[3])
    load_links.start()
    load_turns = pltpu.make_async_copy(turns_in, turns, load_sem.at[4])
    load_turns.start()

    pl.semaphore_wait(barrier, partners)

    def send_pred(piece, patch, to, slot):
        return pltpu.make_async_remote_copy(
            src_ref=pred.at[pl.ds(pl.multiple_of(piece * share, 16), share)],
            dst_ref=pin.at[me],
            send_sem=pred_send.at[slot],
            recv_sem=pin_sem,
            device_id={"patch": patch, "ens": base + to},
            device_id_type=MESH,
        )

    def each_pred(act):
        def across(i, carry):
            piece = lax.rem(me + i, pieces)
            upper = piece >= quarter

            @pl.when(upper & has_right)
            def _():
                act(send_pred(piece, me_p + 1, piece - quarter, pieces + piece))

            @pl.when(jnp.logical_not(upper) & has_left)
            def _():
                act(send_pred(piece, me_p - 1, scorers - quarter + piece, pieces + piece))

            @pl.when(piece + quarter != place)
            def _():
                act(send_pred(piece, me_p, piece + quarter, piece))

            return carry

        lax.fori_loop(0, pieces, across, 0)

    each_pred(lambda copy: copy.start())

    def tell(i, carry):
        @pl.when(i != place)
        def _():
            pl.semaphore_signal(
                ready, inc=1, device_id={"patch": me_p, "ens": base + i}, device_id_type=MESH
            )

        return carry

    lax.fori_loop(0, scorers, tell, 0)

    def tell_across(patch, ens):
        pl.semaphore_signal(
            cross, inc=1, device_id={"patch": patch, "ens": ens}, device_id_type=MESH
        )

    @pl.when(me_p == half + 1)
    def _():
        lax.fori_loop(
            0, relays, lambda i, c: (tell_across(relay_patch(tail_side, i, half), me), c)[1], 0
        )
        lax.fori_loop(
            pieces, pieces + quarter, lambda i, c: (tell_across(half - 1, base + i), c)[1], 0
        )

    def send_target(first, patch):
        return pltpu.make_async_remote_copy(
            src_ref=target.at[pl.ds(pl.multiple_of(first, 16), share)],
            dst_ref=tin,
            send_sem=tgt_send,
            recv_sem=tin_sem,
            device_id={"patch": patch, "ens": me},
            device_id_type=MESH,
        )

    def each_target(act):
        @pl.when(low & has_right)
        def _():
            act(send_target((quarter + jnp.where(low, place, 0)) * share, me_p + 1))

        @pl.when(high & has_left)
        def _():
            act(send_target(jnp.where(high, place - (scorers - quarter), 0) * share, me_p - 1))

    each_target(lambda copy: copy.start())

    @pl.when(middle)
    def _():
        own = pl.ds(pl.multiple_of(jnp.where(middle, place - quarter, 0) * share, 16), share)
        pltpu.make_async_copy(pred.at[own], pin.at[me], pin_sem).start()
        pltpu.make_async_copy(target.at[own], tin, tin_sem).start()

    def send_tail():
        return pltpu.make_async_remote_copy(
            src_ref=h1.at[pl.ds(64, 64)],
            dst_ref=hext.at[pl.ds(0, 64)],
            send_sem=h_send.at[0],
            recv_sem=h_recv.at[0],
            device_id={"patch": me_p + 1, "ens": me},
            device_id_type=MESH,
        )

    def send_head():
        return pltpu.make_async_remote_copy(
            src_ref=h1.at[pl.ds(0, 64)],
            dst_ref=hext.at[pl.ds(192, 64)],
            send_sem=h_send.at[1],
            recv_sem=h_recv.at[1],
            device_id={"patch": me_p - 1, "ens": me},
            device_id_type=MESH,
        )

    def cut(ref, index, first):
        row = lax.rem(index, row_cuts) * piece_rows + first
        column = pl.multiple_of((index // row_cuts) * piece_cols, 128)
        return ref.at[pl.ds(pl.multiple_of(row, 16), piece_rows), pl.ds(column, piece_cols)]

    def to_relay(index, first, side):
        return pltpu.make_async_remote_copy(
            src_ref=cut(h1, index, first),
            dst_ref=relay,
            send_sem=x_send.at[index],
            recv_sem=relay_recv,
            device_id={"patch": relay_patch(side, index, half), "ens": me},
            device_id_type=MESH,
        )

    def each_halo(act):
        @pl.when(has_right)
        def _():
            act(send_tail())

        @pl.when(has_left)
        def _():
            act(send_head())

        @pl.when(me_p == half - 1)
        def _():
            lax.fori_loop(0, relays, lambda i, c: (act(to_relay(i, 64, tail_side)), c)[1], 0)

        @pl.when(me_p == half)
        def _():
            lax.fori_loop(0, relays, lambda i, c: (act(to_relay(i, 0, head_side)), c)[1], 0)

    each_halo(lambda copy: copy.start())

    def onward(index, first, patch, slot):
        return pltpu.make_async_remote_copy(
            src_ref=relay,
            dst_ref=cut(hext, index, first),
            send_sem=relay_send,
            recv_sem=h_recv.at[slot],
            device_id={"patch": patch, "ens": me},
            device_id_type=MESH,
        )

    def forward_tail():
        return onward(jnp.where(tail_relay, tail_index, 0), 0, half, 0)

    def forward_head():
        return onward(jnp.where(head_relay, head_index, 0), 192, half - 1, 1)

    load_links.wait()
    load_turns.wait()
    for first in range(0, 256, 128):
        rows = slice(first, first + 128)
        slots = lax.broadcasted_iota(jnp.int32, (128, 256), 0) + first
        cos_map = jnp.zeros((128, 256), jnp.float32)
        sin_map = jnp.zeros((128, 256), jnp.float32)
        for column in range(K):
            cosine, sine = turn_table(turns[column])
            hit = links[column] == slots
            cos_map += jnp.where(hit, cosine, 0.0)
            sin_map += jnp.where(hit, sine, 0.0)
        tmaps[0, rows] = cos_map.astype(jnp.bfloat16)
        tmaps[1, rows] = sin_map.astype(jnp.bfloat16)
        maps[0, :, rows] = cos_map.T.astype(jnp.bfloat16)
        maps[1, :, rows] = sin_map.T.astype(jnp.bfloat16)

    @pl.when(me_p == 0)
    def _():
        hext[0:64] = jnp.zeros((64, hext.shape[1]), hext.dtype)

    @pl.when(me_p == last)
    def _():
        hext[192:256] = jnp.zeros((64, hext.shape[1]), hext.dtype)

    @pl.when(head_relay)
    def _():
        pltpu.make_async_copy(relay, relay, relay_recv).wait()
        forward_head().start()

    outside = (low & (me_p == 0)) | (high & (me_p == last))

    def side_of(left, right):
        return jnp.where(left > right, 1.0, jnp.where(left < right, -1.0, 0.0))

    def send_grad(to):
        return pltpu.make_async_remote_copy(
            src_ref=gout.at[to],
            dst_ref=gext.at[jnp.where(scorer, place, 0)],
            send_sem=g_send.at[to],
            recv_sem=g_sem,
            device_id={"patch": me_p, "ens": to},
            device_id_type=MESH,
        )

    def each_grad(act):
        def one(to, carry):
            @pl.when(to != me)
            def _():
                act(send_grad(to))

            return carry

        lax.fori_loop(0, members, one, 0)

    def send_across(to, patch, share_index):
        return pltpu.make_async_remote_copy(
            src_ref=gout.at[to],
            dst_ref=gext.at[share_index],
            send_sem=c_send.at[to],
            recv_sem=g_sem,
            device_id={"patch": patch, "ens": to},
            device_id_type=MESH,
        )

    def send_up(i):
        return send_across(i, half, jnp.where(tail_scorer, place - pieces, 0))

    def send_down(i):
        return send_across(i, half - 1, jnp.where(head_scorer, place + pieces, 0))

    idle = (low & over) | (high & under)

    @pl.when(scorer & idle)
    def _():
        pl.semaphore_wait(ready, members - 1)

    @pl.when(scorer & jnp.logical_not(idle))
    def _():
        @pl.when(outside)
        def _():
            pin[...] = jnp.zeros(pin.shape, pin.dtype)
            tin[...] = jnp.zeros(tin.shape, tin.dtype)

        @pl.when(jnp.logical_not(outside))
        def _():
            with jax.named_scope("wait_pred"):
                pltpu.make_async_copy(pin, pin, pin_sem).wait()
                pltpu.make_async_copy(tin, tin, tin_sem).wait()

        with jax.named_scope("score"):
            for first in range(0, share, 16):
                rows = slice(first, first + 16)
                values = pin[:, rows].astype(jnp.float32)
                observed = tin[rows].astype(jnp.float32)
                total = jnp.zeros(values.shape, jnp.float32)
                for shift in range(1, members // 2 + 1):
                    other = jnp.concatenate([values[shift:], values[:shift]], axis=0)
                    side = side_of(values, other)
                    total += side
                    if shift < members // 2:
                        total -= jnp.concatenate(
                            [side[members - shift :], side[: members - shift]], axis=0
                        )
                own_side = side_of(values, observed[None])
                gout[:, rows] = (own_side - total / (members - 1)).astype(jnp.bfloat16)
        with jax.named_scope("send_grad"):

            @pl.when(head_scorer)
            def _():
                lax.fori_loop(0, members, lambda i, c: (send_down(i).start(), c)[1], 0)

            pl.semaphore_wait(ready, members - 1)
            each_grad(lambda copy: copy.start())
            pltpu.make_async_copy(
                gout.at[me], gext.at[jnp.where(scorer, place, 0)], g_sem
            ).start()

    load_w2.wait()
    w2c[0:512, 0:128] = w2v[0:512]
    w2c[0:512, 128:256] = w2v[512:1024]
    w2c[512:1024, 0:128] = w2v[512:1024]
    w2c[512:1024, 128:256] = -w2v[0:512]

    own_h.wait()

    @pl.when(me_p > 0)
    def _():
        pltpu.make_async_copy(hext.at[pl.ds(0, 64)], hext.at[pl.ds(0, 64)], h_recv.at[0]).wait()

    @pl.when(tail_scorer)
    def _():
        pl.semaphore_wait(cross, members)
        lax.fori_loop(0, members, lambda i, c: (send_up(i).start(), c)[1], 0)

    @pl.when(me_p < last)
    def _():
        pltpu.make_async_copy(
            hext.at[pl.ds(192, 64)], hext.at[pl.ds(192, 64)], h_recv.at[1]
        ).wait()

    features = hext[...]
    by_cos = jnp.dot(maps[0, 32:224], features, preferred_element_type=jnp.float32)
    by_sin = jnp.dot(maps[1, 32:224], features, preferred_element_type=jnp.float32)
    summed = jnp.concatenate(
        [
            (by_cos[:, :512] - by_sin[:, 512:]).astype(jnp.bfloat16),
            (by_sin[:, :512] + by_cos[:, 512:]).astype(jnp.bfloat16),
        ],
        axis=1,
    )
    load_w1.wait()
    pre_act = jnp.dot(summed, w1v[...], preferred_element_type=jnp.float32)
    sigmoid = jax.nn.sigmoid(pre_act)
    deriv[...] = sigmoid * (1.0 + pre_act * (1.0 - sigmoid))
    back[0:32] = jnp.zeros((32, back.shape[1]), back.dtype)
    back[224:256] = jnp.zeros((32, back.shape[1]), back.dtype)

    pltpu.make_async_copy(gext, gext, g_sem).wait()
    grads = gext[...].reshape(256, 128)
    spread_grads = jnp.concatenate(
        [
            jnp.dot(tmaps[0, 32:224], grads, preferred_element_type=jnp.float32),
            jnp.dot(tmaps[1, 32:224], grads, preferred_element_type=jnp.float32),
        ],
        axis=1,
    ).astype(jnp.bfloat16)
    contract_last = (((1,), (1,)), ((), ()))
    gmid[...] = lax.dot_general(
        spread_grads, w2c[...], contract_last, preferred_element_type=jnp.float32
    )
    act_grad = (gmid[...] * deriv[...]).astype(jnp.bfloat16)
    back[32:224] = lax.dot_general(
        act_grad, w1v[...], contract_last, preferred_element_type=jnp.float32
    ).astype(jnp.bfloat16)
    rows_back = back[...]
    by_cos = jnp.dot(tmaps[0, 64:192], rows_back, preferred_element_type=jnp.float32)
    by_sin = jnp.dot(tmaps[1, 64:192], rows_back, preferred_element_type=jnp.float32)
    out[:, :512] = (gmid[32:160, :512] + by_cos[:, :512] + by_sin[:, 512:]).astype(out.dtype)
    out[:, 512:] = (gmid[32:160, 512:] + by_cos[:, 512:] - by_sin[:, :512]).astype(out.dtype)

    @pl.when(tail_relay)
    def _():
        pltpu.make_async_copy(relay, relay, relay_recv).wait()
        pl.semaphore_wait(cross, 1)
        forward_tail().start()

    @pl.when(tail_relay)
    def _():
        forward_tail().wait_send()

    @pl.when(head_relay)
    def _():
        forward_head().wait_send()

    @pl.when(tail_scorer)
    def _():
        lax.fori_loop(0, members, lambda i, c: (send_up(i).wait_send(), c)[1], 0)

    @pl.when(head_scorer)
    def _():
        lax.fori_loop(0, members, lambda i, c: (send_down(i).wait_send(), c)[1], 0)

    each_pred(lambda copy: copy.wait_send())
    each_target(lambda copy: copy.wait_send())
    each_halo(lambda copy: copy.wait_send())

    @pl.when(scorer & jnp.logical_not(idle))
    def _():
        each_grad(lambda copy: copy.wait_send())


def per_device(pred, target, h1, w1, w2, neighbours, rotations):
    members = lax.axis_size("ens")
    patches = lax.axis_size("patch")
    rows, channels = h1.shape[1:]
    scorers = members // 2
    share = 256 // scorers
    relays = 4 if patches >= 64 else 1
    row_cuts = min(4, relays)
    anywhere = pl.BlockSpec(memory_space=pltpu.HBM)
    vmem = pl.BlockSpec(memory_space=pltpu.VMEM)
    dma = pltpu.SemaphoreType.DMA
    bf16 = jnp.bfloat16
    result = pl.pallas_call(
        functools.partial(kernel, patches, members),
        out_shape=pltpu.VMEM((rows, channels), bf16),
        in_specs=[anywhere] * 7,
        out_specs=vmem,
        scratch_shapes=[
            pltpu.VMEM((256, channels), bf16),
            pltpu.VMEM((members, share, 128), bf16),
            pltpu.VMEM((share, 128), bf16),
            pltpu.VMEM((members, share, 128), bf16),
            pltpu.VMEM((scorers, share, 128), bf16),
            pltpu.VMEM((channels, channels), bf16),
            pltpu.VMEM((channels, 128), bf16),
            pltpu.VMEM((channels, 256), bf16),
            pltpu.VMEM((2, 256, 256), bf16),
            pltpu.VMEM((2, 256, 256), bf16),
            pltpu.VMEM((192, channels), jnp.float32),
            pltpu.VMEM((192, channels), jnp.float32),
            pltpu.VMEM((256, channels), bf16),
            pltpu.VMEM((64 // row_cuts, channels * row_cuts // relays), bf16),
            dma((5,)),
            dma(()),
            dma(()),
            dma((members,)),
            dma(()),
            dma(()),
            dma((members,)),
            dma((2,)),
            dma((2,)),
            dma((relays,)),
            dma(()),
            dma(()),
            pltpu.SemaphoreType.REGULAR,
            pltpu.SemaphoreType.REGULAR,
            dma((members,)),
            pltpu.VMEM((K, 1, 256), jnp.int32),
            pltpu.VMEM((K, 1, 256), jnp.int32),
        ],
        compiler_params=pltpu.CompilerParams(
            collective_id=0, has_side_effects=True, vmem_limit_bytes=62 * 2**20
        ),
        name="mesh_backward",
    )(
        pred[0],
        target,
        h1[0],
        w1,
        w2,
        jnp.transpose(neighbours, (2, 0, 1)),
        jnp.transpose(rotations, (2, 0, 1)),
    )
    return result[None]


def solution(mesh):
    return jax.shard_map(
        per_device,
        mesh=mesh,
        in_specs=(
            P("ens", "patch", None),
            P("patch", None),
            P("ens", "patch", None),
            P(),
            P(),
            P("patch", None, None),
            P("patch", None, None),
        ),
        out_specs=P("ens", "patch", None),
        check_vma=False,
    )
```
